128 devices in a mesh: lat: 8 (over y, x_lo), lon: 16 (over z, x_hi, core).
Axes of the slice: x: 4 (x_hi: 2, x_lo: 2; x = x_hi * 2 + x_lo), y: 4, z: 4, core: 2. Of those that a mesh axis runs over, the one named last changes fastest.
Arguments:
- control: float32 [120, 512, 4320], P(None, 'lat', 'lon'), may hold values from -6 to 6
- land_mask: int32 [30, 512, 4320], P(None, 'lat', 'lon'), may hold values 0 or 1
- row_class: int32 [512], P('lat'), may hold values from 0 to 15
- decay_rate: float32 [16], replicated, may hold values from 0.004 to 0.05, as said below
- balance: float32 [120, 120], replicated, may hold values from -0.2 to 1.2
Outputs:
- increment: float32 [120, 512, 4320], P(None, 'lat', 'lon')
- velocity: float32 [2, 30, 512, 4320], P(None, None, 'lat', 'lon')
The draws below stay inside these ranges and needn't reach their ends.
Inputs may be any that keep to these rules, and one draw needn't show every extreme that they name: `decay_rate`: a third or more of the entries are 0.02 or more.
All inputs are finite; a program needn't handle non-finite values. No bound on the sum of `land_mask` on one device may be relied on, other than what follows from the above.
Results may differ from the reference program's by a relative error of at most 0.00019.
Values sent between devices are 32-bit elements; how exact they have to be, the bound alone decides.
A program may use at most 192 MiB of HBM per device.

```python
import math
import jax
import jax.numpy as jnp
from jax import lax

LEVELS = 30
VARS = 4
TABLE = 16
COMP = 120
NLAT = 512
NLON = 4320


def draw_decay_rate(key, part):
    key = jax.random.fold_in(key, 11)
    spread = jax.random.uniform(key, (TABLE,), jnp.float32)
    index = jnp.arange(TABLE)
    fast_count = (TABLE + 2) // 3
    lowest = jnp.where(index < fast_count, jnp.float32(math.log(0.02)), jnp.float32(math.log(0.004)))
    span = jnp.float32(math.log(0.05)) - lowest
    rate = jnp.exp(lowest + spread * span)
    rate = jnp.where(index == fast_count, jnp.float32(0.004), rate)
    rate = jnp.where(index == fast_count + 1, jnp.float32(0.05), rate)
    return rate


def draw_balance(key, part):
    key = jax.random.fold_in(key, 12)
    noise = jnp.clip(jax.random.normal(key, (COMP, COMP), jnp.float32), -2.2, 2.2)
    return jnp.eye(COMP, dtype=jnp.float32) + 0.35 * noise / jnp.sqrt(jnp.float32(COMP))


def place_ends(values, stream_key, low, largest):
    extent = values.shape
    index_at = [jax.random.randint(jax.random.fold_in(stream_key, axis), (), 0, extent[axis]) for axis in range(len(extent))]
    values = values.at[tuple(index_at)].set(low)
    longest = extent.index(max(extent))
    index_at[longest] = (index_at[longest] + 1) % extent[longest]
    return values.at[tuple(index_at)].set(largest)


def shard_levels(key, shape, pieces, smallest, largest):
    def one(axis_at, parts):
        steps = jax.random.uniform(jax.random.fold_in(jax.random.fold_in(key, 6), axis_at), (parts,), jnp.float32, smallest / len(pieces), largest / len(pieces))
        return jnp.repeat(jnp.exp(steps), shape[axis_at] // parts).reshape((-1,) + (1,) * (len(shape) - axis_at - 1))

    level = one(*pieces[0])
    for cut in pieces[1:]:
        level = level * one(*cut)
    return level


def normal_values(stream_key, shape, width, bound, shards=(), kind=jnp.bfloat16):
    array = width * jax.random.normal(stream_key, shape, jnp.float32)
    if shards:
        array = array * shard_levels(stream_key, shape, shards, -0.22, 0.18)
    return jnp.clip(array, -bound, bound).astype(kind)


def setup_inputs(seed: int = 0) -> dict:
    splits = jax.random.split(jax.random.key(seed), 6)
    return {
        "control": normal_values(splits[0], (COMP, NLAT, NLON), 1.0, 6.0, ((1, 8), (2, 16)), jnp.float32),
        "land_mask": place_ends((jax.random.randint(splits[1], (LEVELS, NLAT, NLON), 0, 5) < 4).astype(jnp.int32), jax.random.fold_in(splits[1], 1), 0, 1),
        "row_class": place_ends(jax.random.randint(splits[2], (NLAT,), 0, TABLE), jax.random.fold_in(splits[2], 1), 0, TABLE - 1).astype(jnp.int32),
        "decay_rate": draw_decay_rate(jax.random.fold_in(splits[5], 71), 0),
        "balance": draw_balance(jax.random.fold_in(splits[5], 71), 0),
    }


def periodic_pass(field_values, retention_factor, scale_factor, forward_sweep):
    length = field_values.shape[2]
    series = jnp.moveaxis(field_values, 2, 0)

    def advance(carried, inbound_state):
        carried = retention_factor[None, :] * carried + scale_factor[None, :] * inbound_state
        return (carried, carried)
    closing, values = lax.scan(advance, jnp.zeros(series.shape[1:], jnp.float32), series, reverse=not forward_sweep)
    loop_decay = jnp.power(retention_factor, jnp.float32(length))
    wrapped = closing / (1.0 - loop_decay)[None, :]
    offsets = jnp.arange(length, dtype=jnp.float32)
    if forward_sweep:
        exponent = offsets + 1.0
    else:
        exponent = length - offsets
    profile = jnp.power(retention_factor[None, :], exponent[:, None])
    values = values + profile[:, None, :] * wrapped[None]
    return jnp.moveaxis(values, 0, 2)

def open_pass(field_values, retention_factor, scale_factor, forward_sweep):
    series = jnp.moveaxis(field_values, 1, 0)

    def advance(carried, inbound_state):
        column, factor, weight = inbound_state
        carried = factor * carried + weight * column
        return (carried, carried)
    start_state = jnp.zeros((series.shape[1], series.shape[2]), jnp.float32)
    closing, values = lax.scan(advance, start_state, (series, retention_factor, scale_factor), reverse=not forward_sweep)
    return jnp.moveaxis(values, 0, 1)

def reference(control, land_mask, row_class, decay_rate, balance):
    decay = decay_rate[row_class]
    retention_factor = 1.0 - decay
    forward_gain = jnp.sqrt(decay * (2.0 - decay))
    weights = land_mask.astype(jnp.float32)

    def filter_one(field_values):
        masked_in = field_values * weights
        eastward = periodic_pass(masked_in, retention_factor, forward_gain, True)
        westward = periodic_pass(eastward, retention_factor, decay, False)
        northward = open_pass(westward, retention_factor, decay, True)
        southward = open_pass(northward, retention_factor, decay, False)
        return southward * weights
    filtered = lax.map(filter_one, control.reshape(VARS, LEVELS, NLAT, NLON))
    mixed = jnp.dot(balance, filtered.reshape(COMP, NLAT * NLON), precision=lax.Precision.HIGHEST)
    mixed = mixed.reshape(VARS, LEVELS, NLAT, NLON) * weights[None]
    increment = mixed.reshape(COMP, NLAT, NLON)
    pressure = mixed[VARS - 1]
    padded = jnp.pad(pressure, ((0, 0), (1, 1), (0, 0)))
    merid_diff = (padded[:, 2:, :] - padded[:, :-2, :]) * 0.5
    zonal_diff = (jnp.roll(pressure, -1, axis=2) - jnp.roll(pressure, 1, axis=2)) * 0.5
    row_float = jnp.arange(NLAT, dtype=jnp.float32)
    latitude = (-70.0 + 140.0 * (row_float + 0.5) / NLAT) * (math.pi / 180.0)
    sine_lat = jnp.sin(latitude)
    coriolis_inverse = sine_lat / (sine_lat * sine_lat + 0.01)
    east_speed = -coriolis_inverse[None, :, None] * merid_diff * weights
    north_speed = coriolis_inverse[None, :, None] * zonal_diff * weights
    velocity = jnp.stack([east_speed, north_speed])
    return (increment, velocity)
```

```python
import functools
import math

import jax
import jax.numpy as jnp
from jax import lax
from jax.experimental import pallas as pl
from jax.experimental.pallas import tpu as pltpu
from jax.sharding import PartitionSpec as P

COMP = 120
LEVELS = 30
ROWS = 64
SECTOR = 270
LANES = 128
BLOCKS = 3
TAIL = SECTOR - 2 * LANES
CLASSES = 16
PITCH = 136
PRESSURE_PITCH = 40
EXTENT = 272
PADDED = 320
BAND = 16
STRIP = 72
MESH = pl.DeviceIdType.MESH
F32 = jnp.float32
BF16 = jnp.bfloat16
SMEM = pl.BlockSpec(memory_space=pltpu.SMEM)
VMEM = pl.BlockSpec(memory_space=pltpu.VMEM)
LIMIT = 50 * 1024 * 1024


def lane_iota(rows):
    return lax.broadcasted_iota(jnp.int32, (rows, LANES), 1)


def lane_of(value, lane):
    return jnp.broadcast_to(value[:, lane : lane + 1], value.shape)


def class_decay(rate_ref):
    row = lax.broadcasted_iota(jnp.int32, (CLASSES, LANES), 0)
    decay = jnp.zeros((CLASSES, LANES), F32)
    for entry in range(CLASSES):
        decay = jnp.where(row == entry, rate_ref[entry], decay)
    return decay


def split(value):
    high = value.astype(BF16)
    return high, (value - high.astype(F32)).astype(BF16)


def transposed_dot(left, right):
    return lax.dot_general(left, right, (((1,), (1,)), ((), ())), preferred_element_type=F32)


def identity(size):
    shape = (size, size)
    same = lax.broadcasted_iota(jnp.int32, shape, 0) == lax.broadcasted_iota(jnp.int32, shape, 1)
    return same.astype(F32).astype(BF16)


def row_keep(class_ref, rate_ref, first, rows):
    at = lax.broadcasted_iota(jnp.int32, (rows, LANES), 0)
    decay = jnp.zeros((rows, LANES), F32)
    for k in range(rows):
        decay = jnp.where(at == k, rate_ref[class_ref[first + k]], decay)
    return 1.0 - decay


def longitude_kernel(
    class_ref, rate_ref, control_ref, mask_ref, y_ref, ew_ref, q_ref, weight_ref, edge_ref, rim_ref, flat, sea
):
    step = pl.program_id(0)

    @pl.when(step == 0)
    def _():
        flat[...] = jnp.zeros_like(flat)

    lane = lane_iota(8)
    for level in range(LEVELS):
        for part in range(BAND // 8):
            for block in range(BLOCKS):
                weight = mask_ref[level, part * 8 : part * 8 + 8, pl.ds(block * LANES, LANES)].astype(F32)
                if block == BLOCKS - 1:
                    weight = jnp.where(lane < TAIL, weight, 0.0)
                for group in range(4):
                    place = part * 8 * PITCH + group * LEVELS + level
                    flat[block, pl.ds(place, 8, stride=PITCH), :] = weight

    eye = identity(2 * LANES)
    small = eye[:16, :LANES]

    def pair(k, _):
        at = [pl.ds(pl.multiple_of((2 * k + n) * PITCH, 8), LANES) for n in range(2)]
        parts = [
            jnp.concatenate([flat[b, at[n], :] for n in range(2)], axis=0).astype(BF16)
            for b in range(BLOCKS)
        ]
        main = transposed_dot(eye, jnp.concatenate(parts[:2], axis=1))
        tail = transposed_dot(small, parts[2])
        for n in range(2):
            whole = jnp.concatenate(
                [main[:, n * LANES : (n + 1) * LANES], tail[:, n * LANES : (n + 1) * LANES]], axis=0
            )
            row = 2 * k + n
            weight_ref[row] = whole.astype(BF16)
            for t in range(EXTENT // 8):
                sea[pl.ds(t * 8 * BAND + row, 8, stride=BAND), :] = whole[t * 8 : t * 8 + 8]
        return 0

    lax.fori_loop(0, BAND // 2, pair, 0)

    @pl.when(step == 0)
    def _():
        rim_ref[0] = weight_ref[0].astype(F32)

    @pl.when(step == ROWS // BAND - 1)
    def _():
        rim_ref[1] = weight_ref[BAND - 1].astype(F32)

    edge_ref[0] = sea[:BAND]
    edge_ref[1] = sea[(SECTOR - 1) * BAND : SECTOR * BAND]

    keep = row_keep(class_ref, rate_ref, step * BAND, BAND)
    q = keep * keep
    q4 = q * q
    q8 = q4 * q4
    q256 = q8
    for _ in range(5):
        q256 = q256 * q256
    q_ref[...] = q256 * q8 * q4 * q

    def taken(j):
        inside = sea[pl.ds(pl.multiple_of(j * BAND, BAND), BAND), :] != 0.0
        return jnp.where(inside, control_ref[j], 0.0)

    def early(k, carried):
        east, west = carried
        back = SECTOR - 1 - k
        east = keep * east + taken(k)
        y_ref[k] = east
        held = keep * west
        y_ref[back] = held
        return east, held + taken(back)

    def late(k, carried):
        east, west = carried
        back = SECTOR - 1 - k
        east = keep * east + taken(k)
        y_ref[k] = y_ref[k] + east
        held = keep * west
        y_ref[back] = y_ref[back] + held
        return east, held + taken(back)

    zero = jnp.zeros((BAND, LANES), F32)
    half = SECTOR // 2
    carried = lax.fori_loop(0, half, early, (zero, zero), unroll=5)
    east, west = lax.fori_loop(half, SECTOR, late, carried, unroll=5)
    y_ref[SECTOR] = keep * east
    y_ref[SECTOR + 1] = keep * west
    for part in range(BAND // 8):
        ew_ref[2 * part] = east[part * 8 : part * 8 + 8]
        ew_ref[2 * part + 1] = west[part * 8 : part * 8 + 8]


def lon_carry_kernel(ew_ref, q_ref, edge_ref, ab_ref, edges_ref, first, second, send_sem, first_sem, second_sem, edge_sem):
    lat, me, count = lax.axis_index("lat"), lax.axis_index("lon"), 16

    barrier = pltpu.get_barrier_semaphore()

    def greet(k, _):
        pl.semaphore_signal(barrier, inc=1, device_id=(lat, lax.rem(me + k, count)), device_id_type=MESH)
        return 0

    lax.fori_loop(1, count, greet, 0)
    pl.semaphore_wait(barrier, count - 1)

    def to_share(k):
        to = lax.rem(me + k, count)
        return pltpu.make_async_remote_copy(
            src_ref=ew_ref.at[to],
            dst_ref=first.at[me],
            send_sem=send_sem.at[to],
            recv_sem=first_sem.at[me],
            device_id=(lat, to),
            device_id_type=MESH,
        )

    def at_share(k):
        source = lax.rem(me + k, count)
        return pltpu.make_async_remote_copy(
            src_ref=first.at[source],
            dst_ref=first.at[source],
            send_sem=send_sem.at[source],
            recv_sem=first_sem.at[source],
            device_id=(lat, source),
            device_id_type=MESH,
        )

    def edge_copy(side):
        to = lax.rem(me + (count - 1 if side == 0 else 1), count)
        return pltpu.make_async_remote_copy(
            src_ref=edge_ref.at[side],
            dst_ref=edges_ref.at[1 - side],
            send_sem=edge_sem.at[side],
            recv_sem=edge_sem.at[2 + 1 - side],
            device_id=(lat, to),
            device_id_type=MESH,
        )

    lax.fori_loop(1, count, lambda k, c: (to_share(k).start(), c)[1], 0)
    edge_copy(0).start()
    edge_copy(1).start()
    first[me] = ew_ref[me]
    lax.fori_loop(1, count, lambda k, c: (at_share(k).wait_recv(), c)[1], 0)
    lax.fori_loop(1, count, lambda k, c: (to_share(k).wait_send(), c)[1], 0)

    q = q_ref[pl.ds(pl.multiple_of(me // 2 * 8, 8), 8)]
    is_east = jnp.full((8, LANES), me % 2) == 0
    zero = jnp.zeros((8, LANES), F32)
    ahead, behind = [zero], [zero]
    for t in range(count):
        ahead.append(q * ahead[-1] + first[t])
        behind.append(q * behind[-1] + first[count - 1 - t])
    whole = q
    for _ in range(4):
        whole = whole * whole
    closing = jnp.where(is_east, ahead[count], behind[count]) / (1.0 - whole)
    lift, lifts = jnp.ones((8, LANES), F32), []
    for t in range(count):
        lifts.append(lift)
        lift = lift * q
    for t in range(count):
        opened = jnp.where(is_east, ahead[t], behind[count - 1 - t])
        raised = jnp.where(is_east, lifts[t], lifts[count - 1 - t])
        second[t] = opened + raised * closing

    def to_owner(k):
        to = lax.rem(me + k, count)
        return pltpu.make_async_remote_copy(
            src_ref=second.at[to],
            dst_ref=ab_ref.at[me],
            send_sem=send_sem.at[to],
            recv_sem=second_sem.at[me],
            device_id=(lat, to),
            device_id_type=MESH,
        )

    def at_owner(k):
        source = lax.rem(me + k, count)
        return pltpu.make_async_remote_copy(
            src_ref=second.at[source],
            dst_ref=ab_ref.at[source],
            send_sem=send_sem.at[source],
            recv_sem=second_sem.at[source],
            device_id=(lat, source),
            device_id_type=MESH,
        )

    lax.fori_loop(1, count, lambda k, c: (to_owner(k).start(), c)[1], 0)
    ab_ref[me] = second[me]
    lax.fori_loop(1, count, lambda k, c: (at_owner(k).wait_recv(), c)[1], 0)
    lax.fori_loop(1, count, lambda k, c: (to_owner(k).wait_send(), c)[1], 0)
    edge_copy(0).wait()
    edge_copy(1).wait()


def latitude_kernel(class_ref, rate_ref, y_ref, ab_ref, s_ref, closing_ref, response_ref, constants_ref, tables, drive):
    step = pl.program_id(0)
    tiles = STRIP // 8
    row_of = lax.broadcasted_iota(jnp.int32, (8, LANES), 0)
    decay = class_decay(rate_ref)
    log_keep = jnp.log(1.0 - decay)
    drive[...] = decay * jnp.sqrt(decay / (2.0 - decay))
    place = step * STRIP + lax.broadcasted_iota(jnp.int32, (STRIP, LANES), 0)
    ahead = jnp.where(place == SECTOR + 1, 0, place + 1).astype(F32)
    behind = jnp.where(place == SECTOR + 1, SECTOR + 1, jnp.maximum(SECTOR - place, 0)).astype(F32)
    for entry in range(CLASSES):
        tables[entry, 0] = jnp.exp(log_keep[entry : entry + 1] * ahead)
        tables[entry, 1] = jnp.exp(log_keep[entry : entry + 1] * behind)

    def forward(row, carried):
        north, unit = carried[:tiles], carried[tiles]
        entry = class_ref[row]
        keep = 1.0 - rate_ref[entry]
        gain = jnp.broadcast_to(drive[pl.ds(entry, 1), :], (8, LANES))
        at = row // 8 * 2
        a = jnp.broadcast_to(ab_ref[at, pl.ds(row % 8, 1), :], (8, LANES))
        b = jnp.broadcast_to(ab_ref[at + 1, pl.ds(row % 8, 1), :], (8, LANES))
        done = []
        for t in range(tiles):
            rows = pl.ds(t * 8, 8)
            y = y_ref[pl.ds(t * 8 * ROWS + row, 8, stride=ROWS), :]
            y = y + a * tables[entry, 0, rows, :] + b * tables[entry, 1, rows, :]
            done.append(keep * north[t] + gain * y)
            s_ref[row, rows, :] = done[t]
        unit = keep * unit
        response_ref[0, pl.ds(row, 1), :] = unit[:1]
        return (*done, unit)

    zero = jnp.zeros((8, LANES), F32)
    ones = jnp.ones((8, LANES), F32)
    done = lax.fori_loop(0, ROWS, forward, (*[zero] * tiles, ones), unroll=4)
    for t in range(tiles):
        closing_ref[0, pl.ds(t * 8, 8), :] = done[t]
    product = done[tiles]

    def backward(k, carried):
        south, unit, inflow = carried[:tiles], carried[tiles], carried[tiles + 1]
        row = ROWS - 1 - k
        decay = rate_ref[class_ref[row]]
        keep = 1.0 - decay
        done = []
        for t in range(tiles):
            rows = pl.ds(t * 8, 8)
            done.append(keep * south[t] + decay * s_ref[row, rows, :])
            s_ref[row, rows, :] = done[t]
        unit = keep * unit + decay * jnp.broadcast_to(response_ref[0, pl.ds(row, 1), :], (8, LANES))
        inflow = keep * inflow
        response_ref[0, pl.ds(row, 1), :] = unit[:1]
        response_ref[1, pl.ds(row, 1), :] = inflow[:1]
        return (*done, unit, inflow)

    done = lax.fori_loop(0, ROWS, backward, (*[zero] * tiles, zero, ones), unroll=4)
    for t in range(tiles):
        closing_ref[1, pl.ds(t * 8, 8), :] = done[t]
    last = rate_ref[class_ref[ROWS - 1]]
    constants = jnp.where(row_of == 0, product, done[tiles])
    constants = jnp.where(row_of == 2, 1.0 - last, constants)
    constants_ref[...] = jnp.where(row_of == 3, last, constants)


def lat_carry_kernel(
    closing_ref, constants_ref, rim_ref, inflow_ref, below_ref, rims_ref,
    first, second, others, send_sem, first_sem, second_sem, rate_send, rate_sem, rim_sem,
):
    me, lon, count = lax.axis_index("lat"), lax.axis_index("lon"), 8
    share = PADDED // 8

    barrier = pltpu.get_barrier_semaphore()

    def greet(k, _):
        pl.semaphore_signal(barrier, inc=1, device_id=(lax.rem(me + k, count), lon), device_id_type=MESH)
        return 0

    lax.fori_loop(1, count, greet, 0)
    pl.semaphore_wait(barrier, count - 1)

    def part(index):
        return pl.ds(pl.multiple_of(index * share, share), share)

    def to_share(k):
        to = lax.rem(me + k, count)
        return pltpu.make_async_remote_copy(
            src_ref=closing_ref.at[:, part(to)],
            dst_ref=first.at[me],
            send_sem=send_sem.at[to],
            recv_sem=first_sem.at[me],
            device_id=(to, lon),
            device_id_type=MESH,
        )

    def at_share(k):
        source = lax.rem(me + k, count)
        return pltpu.make_async_remote_copy(
            src_ref=first.at[source],
            dst_ref=first.at[source],
            send_sem=send_sem.at[source],
            recv_sem=first_sem.at[source],
            device_id=(source, lon),
            device_id_type=MESH,
        )

    def rate_copy(k, slot):
        to = lax.rem(me + k, count)
        return pltpu.make_async_remote_copy(
            src_ref=constants_ref,
            dst_ref=others.at[slot],
            send_sem=rate_send.at[to],
            recv_sem=rate_sem.at[slot],
            device_id=(to, lon),
            device_id_type=MESH,
        )

    def rim_copy(side):
        to = lax.rem(me + (count - 1 if side == 0 else 1), count)
        return pltpu.make_async_remote_copy(
            src_ref=rim_ref.at[side],
            dst_ref=rims_ref.at[1 - side],
            send_sem=rim_sem.at[side],
            recv_sem=rim_sem.at[2 + 1 - side],
            device_id=(to, lon),
            device_id_type=MESH,
        )

    lax.fori_loop(1, count, lambda k, c: (rate_copy(k, me).start(), c)[1], 0)
    lax.fori_loop(1, count, lambda k, c: (to_share(k).start(), c)[1], 0)
    rim_copy(0).start()
    rim_copy(1).start()
    first[me] = closing_ref[:, part(me)]
    others[me] = constants_ref[...]
    lax.fori_loop(1, count, lambda k, c: (rate_copy(k, lax.rem(me + k, count)).wait_recv(), c)[1], 0)
    lax.fori_loop(1, count, lambda k, c: (at_share(k).wait_recv(), c)[1], 0)
    lax.fori_loop(1, count, lambda k, c: (rate_copy(k, me).wait_send(), c)[1], 0)
    lax.fori_loop(1, count, lambda k, c: (to_share(k).wait_send(), c)[1], 0)

    shape = (share, LANES)
    second[0, 0] = jnp.zeros(shape, F32)
    for t in range(count - 1):
        second[t + 1, 0] = first[t, 0] + others[t, 0:1, :] * second[t, 0]
    second[count - 1, 1] = jnp.zeros(shape, F32)
    for t in range(count - 1, 0, -1):
        second[t - 1, 1] = (
            first[t, 1] + others[t, 1:2, :] * second[t, 0] + others[t, 0:1, :] * second[t, 1]
        )

    def to_owner(k):
        to = lax.rem(me + k, count)
        return pltpu.make_async_remote_copy(
            src_ref=second.at[to],
            dst_ref=inflow_ref.at[:, part(me)],
            send_sem=send_sem.at[to],
            recv_sem=second_sem.at[me],
            device_id=(to, lon),
            device_id_type=MESH,
        )

    def at_owner(k):
        source = lax.rem(me + k, count)
        return pltpu.make_async_remote_copy(
            src_ref=second.at[source],
            dst_ref=inflow_ref.at[:, part(source)],
            send_sem=send_sem.at[source],
            recv_sem=second_sem.at[source],
            device_id=(source, lon),
            device_id_type=MESH,
        )

    lax.fori_loop(1, count, lambda k, c: (to_owner(k).start(), c)[1], 0)
    inflow_ref[:, part(me)] = second[me]
    below = others[lax.rem(me + count - 1, count)]
    below_ref[...] = below * (me > 0).astype(F32)
    lax.fori_loop(1, count, lambda k, c: (at_owner(k).wait_recv(), c)[1], 0)
    lax.fori_loop(1, count, lambda k, c: (to_owner(k).wait_send(), c)[1], 0)
    rim_copy(0).wait()
    rim_copy(1).wait()


def final_kernel(
    s_ref, weight_ref, mask_ref, inflow_ref, response_ref, below_ref, rims_ref, edges_ref, balance_ref,
    increment_ref, velocity_ref, mixer, picker, padded, mixed, sea, pressure, kept, factor,
):
    step = pl.program_id(0)
    lane = lane_iota(8)

    @pl.when(step == 0)
    def _():
        padded[...] = jnp.zeros_like(padded)
        padded[:COMP, :COMP] = balance_ref[...]
        high, low = split(padded[:LANES])
        mixer[:LANES, :LANES] = high
        mixer[:LANES, LANES:] = high
        mixer[LANES:, :LANES] = low
        mixer[LANES:, LANES:] = jnp.zeros_like(low)
        high, low = split(padded[COMP - LEVELS : COMP - LEVELS + 32])
        picker[:32, :LANES] = high
        picker[:32, LANES:] = high
        picker[32:, :LANES] = low
        picker[32:, LANES:] = jnp.zeros_like(low)
        row = lax.axis_index("lat") * ROWS + lax.broadcasted_iota(jnp.int32, (ROWS, LANES), 0)
        latitude = (-70.0 + 140.0 * (row.astype(F32) + 0.5) / 512.0) * (math.pi / 180.0)
        sine = jnp.sin(latitude)
        factor[...] = 0.5 * (sine / (sine * sine + 0.01))

    def operand(field):
        high, low = split(field)
        return jnp.concatenate([high, low], axis=1)

    def pressures(both):
        product = transposed_dot(picker[...], both)
        total = product[:32] + product[32:]
        end = jnp.concatenate([total[:, 2 * LANES :], jnp.zeros((32, 3 * LANES - EXTENT), F32)], axis=1)
        return [total[:, :LANES], total[:, LANES : 2 * LANES], end]

    def rim_row(field, side, row):
        rim = rims_ref[side]
        result = pressures(operand(field * rim))
        shown = transposed_dot(identity(LANES)[:32], rim.astype(BF16))
        shown = jnp.concatenate([shown, jnp.zeros((32, 3 * LANES - EXTENT), F32)], axis=1)
        for b in range(BLOCKS):
            pressure[b, row * PRESSURE_PITCH : row * PRESSURE_PITCH + 32, :] = (
                result[b] * shown[:, b * LANES : (b + 1) * LANES]
            )

    @pl.when(step == 0)
    def _():
        north, south = inflow_ref[0, :EXTENT], inflow_ref[1, :EXTENT]
        first = s_ref[0] + response_ref[0, 0:1, :] * north + response_ref[1, 0:1, :] * south
        rim_row(below_ref[2:3, :] * first + below_ref[3:4, :] * north, 0, 0)

    @pl.when(step == ROWS // 8)
    def _():
        rim_row(inflow_ref[1, :EXTENT], 1, ROWS + 1)

    @pl.when(step < ROWS // 8)
    def _():
        rows = pl.ds(pl.multiple_of(step * 8, 8), 8)
        west, east = edges_ref[0, rows], edges_ref[1, rows]
        for level in range(LEVELS):
            for block in range(BLOCKS):
                weight = mask_ref[level, :, pl.ds(block * LANES, LANES)].astype(F32)
                if block == BLOCKS - 1:
                    weight = jnp.where(lane == TAIL, lane_of(east, level), weight)
                    weight = jnp.where(lane == TAIL + 1, lane_of(west, level), weight)
                sea[block, pl.ds(level, 8, stride=PRESSURE_PITCH), :] = weight

        def one_row(i, _):
            row = step * 8 + i
            h, p = response_ref[0, pl.ds(row, 1), :], response_ref[1, pl.ds(row, 1), :]
            tail = lax.broadcasted_iota(jnp.int32, (8, LANES), 0)
            weight = weight_ref[i].astype(F32)
            e, w = edges_ref[1, pl.ds(row, 1), :], edges_ref[0, pl.ds(row, 1), :]
            end = jnp.where(tail == 6, e, jnp.where(tail == 7, w, weight[EXTENT - 8 :]))
            weight = jnp.concatenate([weight[: EXTENT - 8], end], axis=0)
            field = s_ref[i] + h * inflow_ref[0, :EXTENT] + p * inflow_ref[1, :EXTENT]
            both = operand(field * weight)
            product = transposed_dot(both, mixer[...])
            total = (product[:, :LANES] + product[:, LANES:]) * weight
            for t in range(EXTENT // 8):
                mixed[pl.ds(t * 64 + i, 8, stride=8), :] = total[t * 8 : t * 8 + 8]
            result = pressures(both)
            at = pl.multiple_of((row + 1) * PRESSURE_PITCH, 8)
            for b in range(BLOCKS):
                pressure[b, pl.ds(at, 32), :] = (
                    result[b] * sea[b, pl.ds(pl.multiple_of(i * PRESSURE_PITCH, 8), 32), :]
                )
            return 0

        lax.fori_loop(0, 8, one_row, 0)

        def place(j, _):
            increment_ref[j] = mixed[pl.ds(pl.multiple_of(j * 8, 8), 8), :]
            return 0

        lax.fori_loop(0, SECTOR, place, 0, unroll=10)

    @pl.when(step > 0)
    def _():
        done = step - 1
        base = done * (8 * PRESSURE_PITCH)
        scale = factor[pl.ds(pl.multiple_of(done * 8, 8), 8)]
        for level in range(LEVELS):
            centre = []
            for block in range(BLOCKS):
                below, here, above = [
                    pressure[block, pl.ds(base + k * PRESSURE_PITCH + level, 8, stride=PRESSURE_PITCH), :]
                    for k in range(3)
                ]
                centre.append(here)
                weight = kept[level, :, pl.ds(block * LANES, LANES)].astype(F32)
                velocity_ref[0, level, :, pl.ds(block * LANES, LANES)] = (
                    -scale * (above - below) * weight
                )
            ups = [pltpu.roll(c, LANES - 1, 1) for c in centre]
            downs = [pltpu.roll(c, 1, 1) for c in centre]
            wrap = pltpu.roll(centre[2], LANES - TAIL - 1, 1)
            for block in range(BLOCKS):
                right = ups[block]
                if block < BLOCKS - 1:
                    right = jnp.where(lane == LANES - 1, ups[block + 1], right)
                left = jnp.where(lane == 0, downs[block - 1] if block else wrap, downs[block])
                weight = kept[level, :, pl.ds(block * LANES, LANES)].astype(F32)
                velocity_ref[1, level, :, pl.ds(block * LANES, LANES)] = (
                    scale * (right - left) * weight
                )

    @pl.when(step < ROWS // 8)
    def _():
        kept[...] = mask_ref[...]


def body(control, land_mask, row_class, decay_rate, balance):
    wide = BLOCKS * LANES
    params = functools.partial(pltpu.CompilerParams, vmem_limit_bytes=LIMIT)

    def like(*shape, dtype=F32):
        return jax.ShapeDtypeStruct(shape, dtype)

    columns = jnp.transpose(control, (2, 1, 0))
    y, ew, q, weight, edge, rim = pl.pallas_call(
        longitude_kernel,
        grid=(ROWS // BAND,),
        in_specs=[
            SMEM,
            SMEM,
            pl.BlockSpec((SECTOR, BAND, LANES), lambda g: (0, g, 0)),
            pl.BlockSpec((LEVELS, BAND, wide), lambda g: (0, g, 0)),
        ],
        out_specs=[
            pl.BlockSpec((EXTENT, BAND, LANES), lambda g: (0, g, 0)),
            pl.BlockSpec((BAND // 4, 8, LANES), lambda g: (g, 0, 0)),
            pl.BlockSpec((BAND, LANES), lambda g: (g, 0)),
            pl.BlockSpec((BAND, EXTENT, LANES), lambda g: (g, 0, 0)),
            pl.BlockSpec((2, BAND, LANES), lambda g: (0, g, 0)),
            pl.BlockSpec((2, EXTENT, LANES), lambda g: (0, 0, 0)),
        ],
        out_shape=[
            like(EXTENT, ROWS, LANES),
            like(16, 8, LANES),
            like(ROWS, LANES),
            like(ROWS, EXTENT, LANES, dtype=BF16),
            like(2, ROWS, LANES),
            like(2, EXTENT, LANES),
        ],
        scratch_shapes=[
            pltpu.VMEM((BLOCKS, BAND * PITCH, LANES), F32),
            pltpu.VMEM((EXTENT * BAND, LANES), F32),
        ],
        compiler_params=params(),
        name="longitude",
    )(row_class, decay_rate, columns, land_mask)

    ab, edges = pl.pallas_call(
        lon_carry_kernel,
        in_specs=[VMEM, VMEM, VMEM],
        out_specs=[VMEM, VMEM],
        out_shape=[like(16, 8, LANES), like(2, ROWS, LANES)],
        scratch_shapes=[
            pltpu.VMEM((16, 8, LANES), F32),
            pltpu.VMEM((16, 8, LANES), F32),
            pltpu.SemaphoreType.DMA((16,)),
            pltpu.SemaphoreType.DMA((16,)),
            pltpu.SemaphoreType.DMA((16,)),
            pltpu.SemaphoreType.DMA((4,)),
        ],
        compiler_params=params(collective_id=0, has_side_effects=True),
        name="lon_carry",
    )(ew, q, edge)

    s, closing, response, constants = pl.pallas_call(
        latitude_kernel,
        grid=(pl.cdiv(EXTENT, STRIP),),
        in_specs=[
            SMEM,
            SMEM,
            pl.BlockSpec((STRIP * ROWS, LANES), lambda g: (g, 0)),
            VMEM,
        ],
        out_specs=[
            pl.BlockSpec((ROWS, STRIP, LANES), lambda g: (0, g, 0)),
            pl.BlockSpec((2, STRIP, LANES), lambda g: (0, g, 0)),
            pl.BlockSpec((2, ROWS, LANES), lambda g: (0, 0, 0)),
            pl.BlockSpec((8, LANES), lambda g: (0, 0)),
        ],
        out_shape=[
            like(ROWS, EXTENT, LANES),
            like(2, PADDED, LANES),
            like(2, ROWS, LANES),
            like(8, LANES),
        ],
        scratch_shapes=[
            pltpu.VMEM((CLASSES, 2, STRIP, LANES), F32),
            pltpu.VMEM((CLASSES, LANES), F32),
        ],
        compiler_params=params(),
        name="latitude",
    )(row_class, decay_rate, y.reshape(EXTENT * ROWS, LANES), ab)

    share = PADDED // 8
    inflow, below, rims = pl.pallas_call(
        lat_carry_kernel,
        in_specs=[VMEM, VMEM, VMEM],
        out_specs=[VMEM, VMEM, VMEM],
        out_shape=[like(2, PADDED, LANES), like(8, LANES), like(2, EXTENT, LANES)],
        scratch_shapes=[
            pltpu.VMEM((8, 2, share, LANES), F32),
            pltpu.VMEM((8, 2, share, LANES), F32),
            pltpu.VMEM((8, 8, LANES), F32),
            pltpu.SemaphoreType.DMA((8,)),
            pltpu.SemaphoreType.DMA((8,)),
            pltpu.SemaphoreType.DMA((8,)),
            pltpu.SemaphoreType.DMA((8,)),
            pltpu.SemaphoreType.DMA((8,)),
            pltpu.SemaphoreType.DMA((4,)),
        ],
        compiler_params=params(collective_id=1, has_side_effects=True),
        name="lat_carry",
    )(closing, constants, rim)

    increment, velocity = pl.pallas_call(
        final_kernel,
        grid=(ROWS // 8 + 1,),
        in_specs=[
            pl.BlockSpec((8, EXTENT, LANES), lambda g: (jnp.minimum(g, 7), 0, 0)),
            pl.BlockSpec((8, EXTENT, LANES), lambda g: (jnp.minimum(g, 7), 0, 0)),
            pl.BlockSpec((LEVELS, 8, wide), lambda g: (0, jnp.minimum(g, 7), 0)),
            *[VMEM] * 6,
        ],
        out_specs=[
            pl.BlockSpec((SECTOR, 8, LANES), lambda g: (0, jnp.minimum(g, 7), 0)),
            pl.BlockSpec((2, LEVELS, 8, wide), lambda g: (0, 0, jnp.maximum(g - 1, 0), 0)),
        ],
        out_shape=[like(SECTOR, ROWS, COMP), like(2, LEVELS, ROWS, SECTOR)],
        scratch_shapes=[
            pltpu.VMEM((2 * LANES, 2 * LANES), BF16),
            pltpu.VMEM((64, 2 * LANES), BF16),
            pltpu.VMEM((LANES, LANES), F32),
            pltpu.VMEM((EXTENT * 8, LANES), F32),
            pltpu.VMEM((BLOCKS, 8 * PRESSURE_PITCH, LANES), F32),
            pltpu.VMEM((BLOCKS, (ROWS + 2) * PRESSURE_PITCH, LANES), F32),
            pltpu.VMEM((LEVELS, 8, wide), jnp.int32),
            pltpu.VMEM((ROWS, LANES), F32),
        ],
        compiler_params=params(),
        name="final",
    )(s, weight, land_mask, inflow, response, below, rims, edges, balance)
    return jnp.transpose(increment, (2, 1, 0)), velocity


def solution(mesh):
    return jax.shard_map(
        body,
        mesh=mesh,
        in_specs=(P(None, "lat", "lon"), P(None, "lat", "lon"), P("lat"), P(), P()),
        out_specs=(P(None, "lat", "lon"), P(None, None, "lat", "lon")),
        check_vma=False,
    )
```

```python
import functools
import math

import jax
import jax.numpy as jnp
from jax import lax
from jax.experimental import pallas as pl
from jax.experimental.pallas import tpu as pltpu
from jax.sharding import PartitionSpec as P

COMP = 120
LEVELS = 30
ROWS = 64
SECTOR = 270
LANES = 128
BLOCKS = 3
TAIL = SECTOR - 2 * LANES
CLASSES = 16
PITCH = 136
PRESSURE_PITCH = 40
EXTENT = 272
BAND = 16
BANDS = ROWS // BAND
ROW_PITCH = 72
SEA_PITCH = 24
SHARE = 40
TILES = SHARE // 8
SHARES = 7
PADDED = SHARES * SHARE
LON = 16
LAT = 8
MESH = pl.DeviceIdType.MESH
F32 = jnp.float32
BF16 = jnp.bfloat16
SMEM = pl.BlockSpec(memory_space=pltpu.SMEM)
VMEM = pl.BlockSpec(memory_space=pltpu.VMEM)
LIMIT = 58 * 1024 * 1024


def lane_iota(rows):
    return lax.broadcasted_iota(jnp.int32, (rows, LANES), 1)


def lane_of(value, lane):
    return jnp.broadcast_to(value[:, lane : lane + 1], value.shape)


def class_decay(rate_ref):
    row = lax.broadcasted_iota(jnp.int32, (CLASSES, LANES), 0)
    decay = jnp.zeros((CLASSES, LANES), F32)
    for entry in range(CLASSES):
        decay = jnp.where(row == entry, rate_ref[entry], decay)
    return decay


def split(value):
    high = value.astype(BF16)
    return high, (value - high.astype(F32)).astype(BF16)


def transposed_dot(left, right):
    return lax.dot_general(left, right, (((1,), (1,)), ((), ())), preferred_element_type=F32)


def identity(size):
    shape = (size, size)
    same = lax.broadcasted_iota(jnp.int32, shape, 0) == lax.broadcasted_iota(jnp.int32, shape, 1)
    return same.astype(F32).astype(BF16)


def row_keep(class_ref, rate_ref, first, rows):
    at = lax.broadcasted_iota(jnp.int32, (rows, LANES), 0)
    decay = jnp.zeros((rows, LANES), F32)
    for k in range(rows):
        decay = jnp.where(at == k, rate_ref[class_ref[first + k]], decay)
    return 1.0 - decay


def analysis_kernel(
    class_ref, rate_ref, control_ref, mask_ref,
    weight_ref, s_ref, inflow_ref, response_ref, below_ref, rims_ref, edges_ref,
    flat, sea, columns, field, state, closing, keeps, laps, starts, rates,
    ew, first, second, ab, edge, edges_in, rim, rims_in, constants, others, lat_first, lat_second, inflow_in,
    ew_send, first_sem, second_send, second_sem, edge_send, edge_sem, rim_send, rim_sem,
    rate_send, rate_sem, share_send, share_sem, reply_send, reply_sem, out_sem,
):
    step = pl.program_id(0)
    lat, lon = lax.axis_index("lat"), lax.axis_index("lon")
    barrier = pltpu.get_barrier_semaphore()

    def remote(source, target, send, recv, to):
        return pltpu.make_async_remote_copy(
            src_ref=source, dst_ref=target, send_sem=send, recv_sem=recv, device_id=to, device_id_type=MESH
        )

    def lon_peer(k):
        return lax.rem(lon + k, LON)

    def lat_peer(k):
        return lax.rem(lat + k, LAT)

    def each(count, act):
        lax.fori_loop(1, count, lambda k, c: (act(k), c)[1], 0)

    def closing_copy(index, slot):
        return remote(ew.at[index], first.at[slot], ew_send.at[index], first_sem.at[slot], (lat, index))

    def carry_copy(to, slot):
        return remote(second.at[to], ab.at[slot], second_send.at[to], second_sem.at[slot], (lat, to))

    def edge_copy(side):
        to = lon_peer(LON - 1 if side == 0 else 1)
        return remote(edge.at[side], edges_in.at[1 - side], edge_send.at[side], edge_sem.at[1 - side], (lat, to))

    def rim_copy(side):
        to = lat_peer(LAT - 1 if side == 0 else 1)
        return remote(rim.at[side], rims_in.at[1 - side], rim_send.at[side], rim_sem.at[1 - side], (to, lon))

    def rate_copy(to, slot):
        return remote(constants, others.at[slot], rate_send.at[to], rate_sem.at[slot], (to, lon))

    def part(index):
        return pl.ds(pl.multiple_of(index * SHARE, 8), SHARE)

    def share_copy(index, slot):
        return remote(
            closing.at[:, part(index)], lat_first.at[slot], share_send.at[index], share_sem.at[slot], (index, lon)
        )

    def share_arrival(slot):
        return remote(lat_first.at[slot], lat_first.at[slot], share_send.at[slot], share_sem.at[slot], (slot, lon))

    def reply_copy(to, index):
        return remote(
            lat_second.at[to], inflow_in.at[:, part(index)], reply_send.at[to], reply_sem.at[index], (to, lon)
        )

    def out_copy(index):
        return pltpu.make_async_copy(field.at[:, part(index)], s_ref.at[:, part(index)], out_sem.at[index])

    zero = jnp.zeros((8, LANES), F32)
    ones = jnp.ones((8, LANES), F32)

    @pl.when(step == 0)
    def _():
        each(LON, lambda k: pl.semaphore_signal(barrier, inc=1, device_id=(lat, lon_peer(k)), device_id_type=MESH))
        each(LAT, lambda k: pl.semaphore_signal(barrier, inc=1, device_id=(lat_peer(k), lon), device_id_type=MESH))
        flat[...] = jnp.zeros_like(flat)
        columns[EXTENT * ROW_PITCH :] = jnp.zeros(((PADDED - EXTENT) * ROW_PITCH, LANES), F32)
        state[...] = jnp.zeros_like(state)
        for block in range(ROWS // 8):
            keep = row_keep(class_ref, rate_ref, block * 8, 8)
            keeps[block * 8 : block * 8 + 8] = keep
            q = keep * keep
            q4 = q * q
            q8 = q4 * q4
            q256 = q8
            for _ in range(5):
                q256 = q256 * q256
            laps[block * 8 : block * 8 + 8] = q256 * q8 * q4 * q
        decay = class_decay(rate_ref)
        log_keep = jnp.log(1.0 - decay)
        rates[0] = decay * jnp.sqrt(decay / (2.0 - decay))
        rates[1] = jnp.exp(log_keep * 8.0)
        rates[2] = jnp.exp(log_keep * (SECTOR + 1.0))
        row = lax.broadcasted_iota(jnp.int32, (8, LANES), 0).astype(F32)
        for entry in range(CLASSES):
            log = log_keep[entry : entry + 1]
            for index in range(SHARES):
                starts[index, entry, 0] = jnp.exp(log * (row + (SHARE * index + 1.0)))
                starts[index, entry, 1] = jnp.exp(log * (SECTOR + 8.0 - SHARE * (index + 1.0) - row))

        def onward(i, unit):
            unit = jnp.broadcast_to(keeps[pl.ds(i, 1), :], (8, LANES)) * unit
            response_ref[0, pl.ds(i, 1), :] = unit[:1]
            return unit

        product = lax.fori_loop(0, ROWS, onward, ones, unroll=4)

        def back(k, carried):
            unit, inflow = carried
            i = ROWS - 1 - k
            keep = jnp.broadcast_to(keeps[pl.ds(i, 1), :], (8, LANES))
            unit = keep * unit + (1.0 - keep) * jnp.broadcast_to(response_ref[0, pl.ds(i, 1), :], (8, LANES))
            inflow = keep * inflow
            response_ref[0, pl.ds(i, 1), :] = unit[:1]
            response_ref[1, pl.ds(i, 1), :] = inflow[:1]
            return unit, inflow

        unit, _ = lax.fori_loop(0, ROWS, back, (zero, ones), unroll=4)
        at = lax.broadcasted_iota(jnp.int32, (8, LANES), 0)
        last = jnp.broadcast_to(keeps[ROWS - 1 :], (8, LANES))
        tile = jnp.where(at == 0, product, unit)
        tile = jnp.where(at == 2, last, tile)
        constants[...] = jnp.where(at == 3, 1.0 - last, tile)

    lane = lane_iota(8)
    for level in range(LEVELS):
        for half in range(BAND // 8):
            for block in range(BLOCKS):
                weight = mask_ref[level, half * 8 : half * 8 + 8, pl.ds(block * LANES, LANES)].astype(F32)
                if block == BLOCKS - 1:
                    weight = jnp.where(lane < TAIL, weight, 0.0)
                for group in range(4):
                    place = half * 8 * PITCH + group * LEVELS + level
                    flat[block, pl.ds(place, 8, stride=PITCH), :] = weight

    eye = identity(2 * LANES)
    small = eye[:16, :LANES]

    def pair(k, _):
        at = [pl.ds(pl.multiple_of((2 * k + n) * PITCH, 8), LANES) for n in range(2)]
        parts = [
            jnp.concatenate([flat[b, at[n], :] for n in range(2)], axis=0).astype(BF16)
            for b in range(BLOCKS)
        ]
        main = transposed_dot(eye, jnp.concatenate(parts[:2], axis=1))
        tail = transposed_dot(small, parts[2])
        for n in range(2):
            whole = jnp.concatenate(
                [main[:, n * LANES : (n + 1) * LANES], tail[:, n * LANES : (n + 1) * LANES]], axis=0
            )
            row = 2 * k + n
            weight_ref[row] = whole.astype(BF16)
            for t in range(EXTENT // 8):
                sea[pl.ds(t * 8 * SEA_PITCH + row, 8, stride=SEA_PITCH), :] = whole[t * 8 : t * 8 + 8]
        return 0

    lax.fori_loop(0, BAND // 2, pair, 0, unroll=4)

    here = pl.ds(pl.multiple_of(step * BAND, BAND), BAND)
    edge[0, here] = sea[:BAND]
    edge[1, here] = sea[(SECTOR - 1) * SEA_PITCH : (SECTOR - 1) * SEA_PITCH + BAND]

    keep = keeps[here]
    keep2 = keep * keep

    def taken(j):
        inside = sea[pl.ds(pl.multiple_of(j * SEA_PITCH, 8), BAND), :] != 0.0
        return jnp.where(inside, control_ref[j], 0.0)

    def spot(j):
        return pl.ds(pl.multiple_of(j * ROW_PITCH + step * BAND, 8), BAND)

    def advance(p, carried, add_east, add_west):
        east, west = carried
        j, k = 2 * p, SECTOR - 1 - 2 * p
        x0, x1 = taken(j), taken(j + 1)
        z0, z1 = taken(k), taken(k - 1)
        mid = keep * x0 + x1
        e0 = keep * east + x0
        e1 = keep2 * east + mid
        if add_east:
            columns[spot(j)] = columns[spot(j)] + e0
            columns[spot(j + 1)] = columns[spot(j + 1)] + e1
        else:
            columns[spot(j)] = e0
            columns[spot(j + 1)] = e1
        w0 = keep * west
        w1 = keep2 * west + keep * z0
        if add_west:
            columns[spot(k)] = columns[spot(k)] + w0
            columns[spot(k - 1)] = columns[spot(k - 1)] + w1
        else:
            columns[spot(k)] = w0
            columns[spot(k - 1)] = w1
        return e1, keep2 * west + (keep * z0 + z1)

    nothing = jnp.zeros((BAND, LANES), F32)
    pairs = SECTOR // 2
    carried = lax.fori_loop(
        0, pairs // 2 - 1, lambda p, c: advance(p, c, False, False), (nothing, nothing), unroll=3
    )
    carried = advance(pairs // 2 - 1, carried, False, False)
    carried = advance(pairs // 2, carried, False, True)
    carried = lax.fori_loop(
        pairs // 2 + 1, pairs - 1, lambda p, c: advance(p, c, True, True), carried, unroll=3
    )
    east, west = advance(pairs - 1, carried, True, True)
    columns[spot(SECTOR)] = keep * east
    columns[spot(SECTOR + 1)] = keep * west

    @pl.when(step == 0)
    def _():
        rim[0] = weight_ref[0].astype(F32)
        pl.semaphore_wait(barrier, LON + LAT - 2)
        each(LAT, lambda k: rate_copy(lat_peer(k), lat).start())
        others[lat] = constants[...]
        rim_copy(0).start()

    for half in range(BAND // 8):
        for side, value in enumerate((east, west)):
            index = step * 4 + half * 2 + side
            ew[index] = value[half * 8 : half * 8 + 8]

            @pl.when(index != lon)
            def _():
                closing_copy(index, lon).start()

            @pl.when(index == lon)
            def _():
                first[lon] = value[half * 8 : half * 8 + 8]

    @pl.when(step == BANDS - 1)
    def _():
        rim[1] = weight_ref[BAND - 1].astype(F32)
        edge_copy(0).start()
        edge_copy(1).start()
        rim_copy(1).start()

    owner = lon // 4

    @pl.when((owner == step - 1) | ((step == BANDS - 1) & (owner == step)))
    def _():
        each(LON, lambda k: closing_copy(lon_peer(k), lon_peer(k)).wait_recv())
        q = laps[pl.ds(pl.multiple_of(lon // 2 * 8, 8), 8)]
        is_east = jnp.full((8, LANES), lon % 2) == 0
        ahead, behind = [zero], [zero]
        for t in range(LON):
            ahead.append(q * ahead[-1] + first[t])
            behind.append(q * behind[-1] + first[LON - 1 - t])
        whole = q
        for _ in range(4):
            whole = whole * whole
        end = jnp.where(is_east, ahead[LON], behind[LON]) / (1.0 - whole)
        lift, lifts = ones, []
        for t in range(LON):
            lifts.append(lift)
            lift = lift * q
        for t in range(LON):
            opened = jnp.where(is_east, ahead[t], behind[LON - 1 - t])
            raised = jnp.where(is_east, lifts[t], lifts[LON - 1 - t])
            second[t] = opened + raised * end
        each(LON, lambda k: carry_copy(lon_peer(k), lon).start())
        ab[lon] = second[lon]

    special = lax.broadcasted_iota(jnp.int32, (8, LANES), 0) == 7

    def forward_band(band, _):
        def arrive(n, c):
            index = band * 4 + n

            @pl.when(index != lon)
            def _():
                carry_copy(index, index).wait_recv()

            return c

        lax.fori_loop(0, 4, arrive, 0)

        def strip(index, _):
            final = special & (jnp.full((8, LANES), index) == SHARES - 1)
            base = pl.multiple_of(index * SHARE, 8)

            def one_row(ii, north):
                row = band * BAND + ii
                entry = class_ref[row]
                keep = 1.0 - rate_ref[entry]
                gain, stride8, far = [
                    jnp.broadcast_to(rates[n, pl.ds(entry, 1), :], (8, LANES)) for n in range(3)
                ]
                at = row // 8 * 2
                a = jnp.broadcast_to(ab[at, pl.ds(row % 8, 1), :], (8, LANES))
                b = jnp.broadcast_to(ab[at + 1, pl.ds(row % 8, 1), :], (8, LANES))
                ahead = [a * starts[index, entry, 0]]
                behind = [b * starts[index, entry, 1]]
                for _ in range(TILES - 1):
                    ahead.append(ahead[-1] * stride8)
                    behind.append(behind[-1] * stride8)
                behind = behind[::-1]
                ahead[3] = jnp.where(final, a, ahead[3])
                behind[3] = jnp.where(final, b * far, behind[3])
                done = []
                for t in range(TILES):
                    y = columns[pl.ds((base + t * 8) * ROW_PITCH + row, 8, stride=ROW_PITCH), :]
                    done.append(keep * north[t] + gain * (y + ahead[t] + behind[t]))
                    field[row, pl.ds(base + t * 8, 8), :] = done[t]
                return tuple(done)

            north = tuple(state[pl.ds(base + t * 8, 8), :] for t in range(TILES))
            north = lax.fori_loop(0, BAND, one_row, north, unroll=4)
            for t in range(TILES):
                state[pl.ds(base + t * 8, 8), :] = north[t]
            return 0

        lax.fori_loop(0, SHARES, strip, 0)
        return 0

    lax.fori_loop(
        jnp.where(step == BANDS - 1, 1, 0),
        jnp.where(step == BANDS - 1, BANDS, jnp.where(step == BANDS - 2, 1, 0)),
        forward_band,
        0,
    )

    @pl.when(step == BANDS - 1)
    def _():
        closing[0] = state[...]
        each(LAT, lambda k: rate_copy(lat_peer(k), lat_peer(k)).wait_recv())

        def strip(index, _):
            base = pl.multiple_of(index * SHARE, 8)

            def one_row(k, south):
                row = ROWS - 1 - k
                decay = rate_ref[class_ref[row]]
                keep = 1.0 - decay
                done = []
                for t in range(TILES):
                    at = pl.ds(base + t * 8, 8)
                    done.append(keep * south[t] + decay * field[row, at, :])
                    field[row, at, :] = done[t]
                return tuple(done)

            south = lax.fori_loop(0, ROWS, one_row, (zero,) * TILES, unroll=4)
            for t in range(TILES):
                closing[1, pl.ds(base + t * 8, 8), :] = south[t]
            out_copy(index).start()

            @pl.when(index != lat)
            def _():
                share_copy(index, lat).start()

            @pl.when(index == lat)
            def _():
                lat_first[lat] = closing[:, part(lat)]

            @pl.when((lat < SHARES) & (index == jnp.minimum(lat + 2, SHARES - 1)))
            def _():
                each(LAT, lambda k: share_arrival(lat_peer(k)).wait_recv())
                blank = jnp.zeros((SHARE, LANES), F32)
                lat_second[0, 0] = blank
                for t in range(LAT - 1):
                    lat_second[t + 1, 0] = lat_first[t, 0] + others[t, 0:1, :] * lat_second[t, 0]
                lat_second[LAT - 1, 1] = blank
                for t in range(LAT - 1, 0, -1):
                    lat_second[t - 1, 1] = (
                        lat_first[t, 1]
                        + others[t, 1:2, :] * lat_second[t, 0]
                        + others[t, 0:1, :] * lat_second[t, 1]
                    )
                each(LAT, lambda k: reply_copy(lat_peer(k), lat).start())
                inflow_in[:, part(lat)] = lat_second[lat]

            return 0

        lax.fori_loop(0, SHARES, strip, 0)
        edge_copy(0).wait()
        edge_copy(1).wait()
        rim_copy(0).wait()
        rim_copy(1).wait()
        edges_ref[...] = edges_in[...]
        rims_ref[...] = rims_in[...]
        below_ref[...] = others[lat_peer(LAT - 1)] * (lat > 0).astype(F32)
        each(LON, lambda k: closing_copy(lon_peer(k), lon).wait_send())
        each(LON, lambda k: carry_copy(lon_peer(k), lon).wait_send())
        each(LAT, lambda k: rate_copy(lat_peer(k), lat).wait_send())

        def settle(index, c):
            @pl.when(index != lat)
            def _():
                share_copy(index, lat).wait_send()
                reply_copy(index, index).wait_recv()

            out_copy(index).wait()
            return c

        lax.fori_loop(0, SHARES, settle, 0)

        @pl.when(lat < SHARES)
        def _():
            each(LAT, lambda k: reply_copy(lat_peer(k), lat).wait_send())

        inflow_ref[...] = inflow_in[...]


def final_kernel(
    s_ref, weight_ref, mask_ref, inflow_ref, response_ref, below_ref, rims_ref, edges_ref, balance_ref,
    increment_ref, velocity_ref, mixer, picker, padded, mixed, sea, pressure, kept, factor,
):
    step = pl.program_id(0)
    lane = lane_iota(8)

    @pl.when(step == 0)
    def _():
        padded[...] = jnp.zeros_like(padded)
        padded[:COMP, :COMP] = balance_ref[...]
        high, low = split(padded[:LANES])
        mixer[:LANES, :LANES] = high
        mixer[:LANES, LANES:] = high
        mixer[LANES:, :LANES] = low
        mixer[LANES:, LANES:] = jnp.zeros_like(low)
        high, low = split(padded[COMP - LEVELS : COMP - LEVELS + 32])
        picker[:32, :LANES] = high
        picker[:32, LANES:] = high
        picker[32:, :LANES] = low
        picker[32:, LANES:] = jnp.zeros_like(low)
        row = lax.axis_index("lat") * ROWS + lax.broadcasted_iota(jnp.int32, (ROWS, LANES), 0)
        latitude = (-70.0 + 140.0 * (row.astype(F32) + 0.5) / 512.0) * (math.pi / 180.0)
        sine = jnp.sin(latitude)
        factor[...] = 0.5 * (sine / (sine * sine + 0.01))

    def operand(field):
        high, low = split(field)
        return jnp.concatenate([high, low], axis=1)

    def pressures(both):
        product = transposed_dot(picker[...], both)
        total = product[:32] + product[32:]
        end = jnp.concatenate([total[:, 2 * LANES :], jnp.zeros((32, 3 * LANES - EXTENT), F32)], axis=1)
        return [total[:, :LANES], total[:, LANES : 2 * LANES], end]

    def rim_row(field, side, row):
        rim = rims_ref[side]
        result = pressures(operand(field * rim))
        shown = transposed_dot(identity(LANES)[:32], rim.astype(BF16))
        shown = jnp.concatenate([shown, jnp.zeros((32, 3 * LANES - EXTENT), F32)], axis=1)
        for b in range(BLOCKS):
            pressure[b, row * PRESSURE_PITCH : row * PRESSURE_PITCH + 32, :] = (
                result[b] * shown[:, b * LANES : (b + 1) * LANES]
            )

    @pl.when(step == 0)
    def _():
        north, south = inflow_ref[0, :EXTENT], inflow_ref[1, :EXTENT]
        first = s_ref[0] + response_ref[0, 0:1, :] * north + response_ref[1, 0:1, :] * south
        rim_row(below_ref[2:3, :] * first + below_ref[3:4, :] * north, 0, 0)

    @pl.when(step == ROWS // 8)
    def _():
        rim_row(inflow_ref[1, :EXTENT], 1, ROWS + 1)

    @pl.when(step < ROWS // 8)
    def _():
        rows = pl.ds(pl.multiple_of(step * 8, 8), 8)
        west, east = edges_ref[0, rows], edges_ref[1, rows]
        for level in range(LEVELS):
            for block in range(BLOCKS):
                weight = mask_ref[level, :, pl.ds(block * LANES, LANES)].astype(F32)
                if block == BLOCKS - 1:
                    weight = jnp.where(lane == TAIL, lane_of(east, level), weight)
                    weight = jnp.where(lane == TAIL + 1, lane_of(west, level), weight)
                sea[block, pl.ds(level, 8, stride=PRESSURE_PITCH), :] = weight

        def one_row(i, _):
            row = step * 8 + i
            h, p = response_ref[0, pl.ds(row, 1), :], response_ref[1, pl.ds(row, 1), :]
            tail = lax.broadcasted_iota(jnp.int32, (8, LANES), 0)
            weight = weight_ref[i].astype(F32)
            e, w = edges_ref[1, pl.ds(row, 1), :], edges_ref[0, pl.ds(row, 1), :]
            end = jnp.where(tail == 6, e, jnp.where(tail == 7, w, weight[EXTENT - 8 :]))
            weight = jnp.concatenate([weight[: EXTENT - 8], end], axis=0)
            field = s_ref[i] + h * inflow_ref[0, :EXTENT] + p * inflow_ref[1, :EXTENT]
            both = operand(field * weight)
            product = transposed_dot(both, mixer[...])
            total = (product[:, :LANES] + product[:, LANES:]) * weight
            for t in range(EXTENT // 8):
                mixed[pl.ds(t * 64 + i, 8, stride=8), :] = total[t * 8 : t * 8 + 8]
            result = pressures(both)
            at = pl.multiple_of((row + 1) * PRESSURE_PITCH, 8)
            for b in range(BLOCKS):
                pressure[b, pl.ds(at, 32), :] = (
                    result[b] * sea[b, pl.ds(pl.multiple_of(i * PRESSURE_PITCH, 8), 32), :]
                )
            return 0

        lax.fori_loop(0, 8, one_row, 0, unroll=4)

        def place(j, _):
            increment_ref[j] = mixed[pl.ds(pl.multiple_of(j * 8, 8), 8), :]
            return 0

        lax.fori_loop(0, SECTOR, place, 0, unroll=10)

    @pl.when(step > 0)
    def _():
        done = step - 1
        base = done * (8 * PRESSURE_PITCH)
        scale = factor[pl.ds(pl.multiple_of(done * 8, 8), 8)]
        for level in range(LEVELS):
            centre = []
            for block in range(BLOCKS):
                below, here, above = [
                    pressure[block, pl.ds(base + k * PRESSURE_PITCH + level, 8, stride=PRESSURE_PITCH), :]
                    for k in range(3)
                ]
                centre.append(here)
                weight = kept[level, :, pl.ds(block * LANES, LANES)].astype(F32)
                velocity_ref[0, level, :, pl.ds(block * LANES, LANES)] = (
                    -scale * (above - below) * weight
                )
            ups = [pltpu.roll(c, LANES - 1, 1) for c in centre]
            downs = [pltpu.roll(c, 1, 1) for c in centre]
            wrap = pltpu.roll(centre[2], LANES - TAIL - 1, 1)
            for block in range(BLOCKS):
                right = ups[block]
                if block < BLOCKS - 1:
                    right = jnp.where(lane == LANES - 1, ups[block + 1], right)
                left = jnp.where(lane == 0, downs[block - 1] if block else wrap, downs[block])
                weight = kept[level, :, pl.ds(block * LANES, LANES)].astype(F32)
                velocity_ref[1, level, :, pl.ds(block * LANES, LANES)] = (
                    scale * (right - left) * weight
                )

    @pl.when(step < ROWS // 8)
    def _():
        kept[...] = mask_ref[...]


def body(control, land_mask, row_class, decay_rate, balance):
    wide = BLOCKS * LANES
    params = functools.partial(pltpu.CompilerParams, vmem_limit_bytes=LIMIT)

    def like(*shape, dtype=F32):
        return jax.ShapeDtypeStruct(shape, dtype)

    columns = jnp.transpose(control, (2, 1, 0))

    dma = pltpu.SemaphoreType.DMA
    fixed2, fixed3 = (lambda g: (0, 0)), (lambda g: (0, 0, 0))
    weight, s, inflow, response, below, rims, edges = pl.pallas_call(
        analysis_kernel,
        grid=(BANDS,),
        in_specs=[
            SMEM,
            SMEM,
            pl.BlockSpec((SECTOR, BAND, LANES), lambda g: (0, g, 0)),
            pl.BlockSpec((LEVELS, BAND, wide), lambda g: (0, g, 0)),
        ],
        out_specs=[
            pl.BlockSpec((BAND, EXTENT, LANES), lambda g: (g, 0, 0)),
            pl.BlockSpec(memory_space=pl.ANY),
            pl.BlockSpec((2, PADDED, LANES), fixed3),
            pl.BlockSpec((2, ROWS, LANES), fixed3),
            pl.BlockSpec((8, LANES), fixed2),
            pl.BlockSpec((2, EXTENT, LANES), fixed3),
            pl.BlockSpec((2, ROWS, LANES), fixed3),
        ],
        out_shape=[
            like(ROWS, EXTENT, LANES, dtype=BF16),
            like(ROWS, PADDED, LANES),
            like(2, PADDED, LANES),
            like(2, ROWS, LANES),
            like(8, LANES),
            like(2, EXTENT, LANES),
            like(2, ROWS, LANES),
        ],
        scratch_shapes=[
            pltpu.VMEM((BLOCKS, BAND * PITCH, LANES), F32),
            pltpu.VMEM((EXTENT * SEA_PITCH, LANES), F32),
            pltpu.VMEM((PADDED * ROW_PITCH, LANES), F32),
            pltpu.VMEM((ROWS, PADDED, LANES), F32),
            pltpu.VMEM((PADDED, LANES), F32),
            pltpu.VMEM((2, PADDED, LANES), F32),
            pltpu.VMEM((ROWS, LANES), F32),
            pltpu.VMEM((ROWS, LANES), F32),
            pltpu.VMEM((SHARES, CLASSES, 2, 8, LANES), F32),
            pltpu.VMEM((3, CLASSES, LANES), F32),
            pltpu.VMEM((LON, 8, LANES), F32),
            pltpu.VMEM((LON, 8, LANES), F32),
            pltpu.VMEM((LON, 8, LANES), F32),
            pltpu.VMEM((LON, 8, LANES), F32),
            pltpu.VMEM((2, ROWS, LANES), F32),
            pltpu.VMEM((2, ROWS, LANES), F32),
            pltpu.VMEM((2, EXTENT, LANES), F32),
            pltpu.VMEM((2, EXTENT, LANES), F32),
            pltpu.VMEM((8, LANES), F32),
            pltpu.VMEM((LAT, 8, LANES), F32),
            pltpu.VMEM((LAT, 2, SHARE, LANES), F32),
            pltpu.VMEM((LAT, 2, SHARE, LANES), F32),
            pltpu.VMEM((2, PADDED, LANES), F32),
            dma((LON,)),
            dma((LON,)),
            dma((LON,)),
            dma((LON,)),
            dma((2,)),
            dma((2,)),
            dma((2,)),
            dma((2,)),
            dma((LAT,)),
            dma((LAT,)),
            dma((LAT,)),
            dma((LAT,)),
            dma((LAT,)),
            dma((LAT,)),
            dma((SHARES,)),
        ],
        compiler_params=params(collective_id=0, has_side_effects=True),
        name="analysis",
    )(row_class, decay_rate, columns, land_mask)

    increment, velocity = pl.pallas_call(
        final_kernel,
        grid=(ROWS // 8 + 1,),
        in_specs=[
            pl.BlockSpec((8, EXTENT, LANES), lambda g: (jnp.minimum(g, 7), 0, 0)),
            pl.BlockSpec((8, EXTENT, LANES), lambda g: (jnp.minimum(g, 7), 0, 0)),
            pl.BlockSpec((LEVELS, 8, wide), lambda g: (0, jnp.minimum(g, 7), 0)),
            *[VMEM] * 6,
        ],
        out_specs=[
            pl.BlockSpec((SECTOR, 8, LANES), lambda g: (0, jnp.minimum(g, 7), 0)),
            pl.BlockSpec((2, LEVELS, 8, wide), lambda g: (0, 0, jnp.maximum(g - 1, 0), 0)),
        ],
        out_shape=[like(SECTOR, ROWS, COMP), like(2, LEVELS, ROWS, SECTOR)],
        scratch_shapes=[
            pltpu.VMEM((2 * LANES, 2 * LANES), BF16),
            pltpu.VMEM((64, 2 * LANES), BF16),
            pltpu.VMEM((LANES, LANES), F32),
            pltpu.VMEM((EXTENT * 8, LANES), F32),
            pltpu.VMEM((BLOCKS, 8 * PRESSURE_PITCH, LANES), F32),
            pltpu.VMEM((BLOCKS, (ROWS + 2) * PRESSURE_PITCH, LANES), F32),
            pltpu.VMEM((LEVELS, 8, wide), jnp.int32),
            pltpu.VMEM((ROWS, LANES), F32),
        ],
        compiler_params=params(),
        name="final",
    )(s, weight, land_mask, inflow, response, below, rims, edges, balance)
    return jnp.transpose(increment, (2, 1, 0)), velocity


def solution(mesh):
    return jax.shard_map(
        body,
        mesh=mesh,
        in_specs=(P(None, "lat", "lon"), P(None, "lat", "lon"), P("lat"), P(), P()),
        out_specs=(P(None, "lat", "lon"), P(None, None, "lat", "lon")),
        check_vma=False,
    )
```

```python
import functools
import math

import jax
import jax.numpy as jnp
from jax import lax
from jax.experimental import pallas as pl
from jax.experimental.pallas import tpu as pltpu
from jax.sharding import PartitionSpec as P

COMP = 120
LEVELS = 30
ROWS = 64
SECTOR = 270
LANES = 128
BLOCKS = 3
TAIL = SECTOR - 2 * LANES
CLASSES = 16
PITCH = 136
PRESSURE_PITCH = 40
EXTENT = 272
BAND = 16
BANDS = ROWS // BAND
ROW_PITCH = 72
SEA_PITCH = 24
SHARE = 40
TILES = SHARE // 8
SHARES = 7
PADDED = SHARES * SHARE
LON = 16
LAT = 8
MESH = pl.DeviceIdType.MESH
F32 = jnp.float32
BF16 = jnp.bfloat16
SMEM = pl.BlockSpec(memory_space=pltpu.SMEM)
VMEM = pl.BlockSpec(memory_space=pltpu.VMEM)
LIMIT = 58 * 1024 * 1024


def lane_iota(rows):
    return lax.broadcasted_iota(jnp.int32, (rows, LANES), 1)


def lane_of(value, lane):
    return jnp.broadcast_to(value[:, lane : lane + 1], value.shape)


def class_decay(rate_ref):
    row = lax.broadcasted_iota(jnp.int32, (CLASSES, LANES), 0)
    decay = jnp.zeros((CLASSES, LANES), F32)
    for entry in range(CLASSES):
        decay = jnp.where(row == entry, rate_ref[entry], decay)
    return decay


def split(value):
    high = value.astype(BF16)
    return high, (value - high.astype(F32)).astype(BF16)


def transposed_dot(left, right):
    return lax.dot_general(left, right, (((1,), (1,)), ((), ())), preferred_element_type=F32)


def identity(size):
    shape = (size, size)
    same = lax.broadcasted_iota(jnp.int32, shape, 0) == lax.broadcasted_iota(jnp.int32, shape, 1)
    return same.astype(F32).astype(BF16)


def row_keep(class_ref, rate_ref, first, rows):
    at = lax.broadcasted_iota(jnp.int32, (rows, LANES), 0)
    decay = jnp.zeros((rows, LANES), F32)
    for k in range(rows):
        decay = jnp.where(at == k, rate_ref[class_ref[first + k]], decay)
    return 1.0 - decay


def analysis_kernel(
    class_ref, rate_ref, control_ref, mask_ref,
    weight_ref, s_ref, inflow_ref, response_ref, below_ref, rims_ref, edges_ref,
    flat, sea, columns, field, state, closing, keeps, laps, starts, rates,
    ew, gathered, ab, edge, edges_in, rim, rims_in, constants, others, lat_first, lat_second, inflow_in,
    ew_send, ew_sem, edge_send, edge_sem, rim_send, rim_sem,
    rate_send, rate_sem, share_send, share_sem, reply_send, reply_sem, out_sem,
):
    step = pl.program_id(0)
    lat, lon = lax.axis_index("lat"), lax.axis_index("lon")
    barrier = pltpu.get_barrier_semaphore()

    def remote(source, target, send, recv, to):
        return pltpu.make_async_remote_copy(
            src_ref=source, dst_ref=target, send_sem=send, recv_sem=recv, device_id=to, device_id_type=MESH
        )

    def lon_peer(k):
        return lax.rem(lon + k, LON)

    def lat_peer(k):
        return lax.rem(lat + k, LAT)

    def each(count, act):
        lax.fori_loop(1, count, lambda k, c: (act(k), c)[1], 0)

    def closing_copy(band, to, slot):
        return remote(ew.at[band], gathered.at[band, slot], ew_send.at[band, to], ew_sem.at[band, slot], (lat, to))

    def edge_copy(side):
        to = lon_peer(LON - 1 if side == 0 else 1)
        return remote(edge.at[side], edges_in.at[1 - side], edge_send.at[side], edge_sem.at[1 - side], (lat, to))

    def rim_copy(side):
        to = lat_peer(LAT - 1 if side == 0 else 1)
        return remote(rim.at[side], rims_in.at[1 - side], rim_send.at[side], rim_sem.at[1 - side], (to, lon))

    def rate_copy(to, slot):
        return remote(constants, others.at[slot], rate_send.at[to], rate_sem.at[slot], (to, lon))

    def part(index):
        return pl.ds(pl.multiple_of(index * SHARE, 8), SHARE)

    def share_copy(index, slot):
        return remote(
            closing.at[:, part(index)], lat_first.at[slot], share_send.at[index], share_sem.at[slot], (index, lon)
        )

    def share_arrival(slot):
        return remote(lat_first.at[slot], lat_first.at[slot], share_send.at[slot], share_sem.at[slot], (slot, lon))

    def reply_copy(to, index):
        return remote(
            lat_second.at[to], inflow_in.at[:, part(index)], reply_send.at[to], reply_sem.at[index], (to, lon)
        )

    def out_copy(index):
        return pltpu.make_async_copy(field.at[:, part(index)], s_ref.at[:, part(index)], out_sem.at[index])

    zero = jnp.zeros((8, LANES), F32)
    ones = jnp.ones((8, LANES), F32)

    @pl.when(step == 0)
    def _():
        each(LON, lambda k: pl.semaphore_signal(barrier, inc=1, device_id=(lat, lon_peer(k)), device_id_type=MESH))
        each(LAT, lambda k: pl.semaphore_signal(barrier, inc=1, device_id=(lat_peer(k), lon), device_id_type=MESH))
        flat[...] = jnp.zeros_like(flat)
        columns[EXTENT * ROW_PITCH :] = jnp.zeros(((PADDED - EXTENT) * ROW_PITCH, LANES), F32)
        state[...] = jnp.zeros_like(state)
        for block in range(ROWS // 8):
            keep = row_keep(class_ref, rate_ref, block * 8, 8)
            keeps[block * 8 : block * 8 + 8] = keep
            q = keep * keep
            q4 = q * q
            q8 = q4 * q4
            q256 = q8
            for _ in range(5):
                q256 = q256 * q256
            laps[block * 8 : block * 8 + 8] = q256 * q8 * q4 * q
        decay = class_decay(rate_ref)
        log_keep = jnp.log(1.0 - decay)
        rates[0] = decay * jnp.sqrt(decay / (2.0 - decay))
        rates[1] = jnp.exp(log_keep * 8.0)
        rates[2] = jnp.exp(log_keep * (SECTOR + 1.0))
        row = lax.broadcasted_iota(jnp.int32, (8, LANES), 0).astype(F32)
        for entry in range(CLASSES):
            log = log_keep[entry : entry + 1]
            for index in range(SHARES):
                starts[index, entry, 0] = jnp.exp(log * (row + (SHARE * index + 1.0)))
                starts[index, entry, 1] = jnp.exp(log * (SECTOR + 8.0 - SHARE * (index + 1.0) - row))

        def onward(i, unit):
            unit = jnp.broadcast_to(keeps[pl.ds(i, 1), :], (8, LANES)) * unit
            response_ref[0, pl.ds(i, 1), :] = unit[:1]
            return unit

        product = lax.fori_loop(0, ROWS, onward, ones, unroll=4)

        def back(k, carried):
            unit, inflow = carried
            i = ROWS - 1 - k
            keep = jnp.broadcast_to(keeps[pl.ds(i, 1), :], (8, LANES))
            unit = keep * unit + (1.0 - keep) * jnp.broadcast_to(response_ref[0, pl.ds(i, 1), :], (8, LANES))
            inflow = keep * inflow
            response_ref[0, pl.ds(i, 1), :] = unit[:1]
            response_ref[1, pl.ds(i, 1), :] = inflow[:1]
            return unit, inflow

        unit, _ = lax.fori_loop(0, ROWS, back, (zero, ones), unroll=4)
        at = lax.broadcasted_iota(jnp.int32, (8, LANES), 0)
        last = jnp.broadcast_to(keeps[ROWS - 1 :], (8, LANES))
        tile = jnp.where(at == 0, product, unit)
        tile = jnp.where(at == 2, last, tile)
        constants[...] = jnp.where(at == 3, 1.0 - last, tile)

    lane = lane_iota(8)
    for level in range(LEVELS):
        for half in range(BAND // 8):
            for block in range(BLOCKS):
                weight = mask_ref[level, half * 8 : half * 8 + 8, pl.ds(block * LANES, LANES)].astype(F32)
                if block == BLOCKS - 1:
                    weight = jnp.where(lane < TAIL, weight, 0.0)
                for group in range(4):
                    place = half * 8 * PITCH + group * LEVELS + level
                    flat[block, pl.ds(place, 8, stride=PITCH), :] = weight

    eye = identity(2 * LANES)
    small = eye[:16, :LANES]

    def pair(k, _):
        at = [pl.ds(pl.multiple_of((2 * k + n) * PITCH, 8), LANES) for n in range(2)]
        parts = [
            jnp.concatenate([flat[b, at[n], :] for n in range(2)], axis=0).astype(BF16)
            for b in range(BLOCKS)
        ]
        main = transposed_dot(eye, jnp.concatenate(parts[:2], axis=1))
        tail = transposed_dot(small, parts[2])
        for n in range(2):
            whole = jnp.concatenate(
                [main[:, n * LANES : (n + 1) * LANES], tail[:, n * LANES : (n + 1) * LANES]], axis=0
            )
            row = 2 * k + n
            weight_ref[row] = whole.astype(BF16)
            for t in range(EXTENT // 8):
                sea[pl.ds(t * 8 * SEA_PITCH + row, 8, stride=SEA_PITCH), :] = whole[t * 8 : t * 8 + 8]
        return 0

    lax.fori_loop(0, BAND // 2, pair, 0, unroll=4)

    here = pl.ds(pl.multiple_of(step * BAND, BAND), BAND)
    edge[0, here] = sea[:BAND]
    edge[1, here] = sea[(SECTOR - 1) * SEA_PITCH : (SECTOR - 1) * SEA_PITCH + BAND]

    keep = keeps[here]
    keep2 = keep * keep

    def taken(j):
        inside = sea[pl.ds(pl.multiple_of(j * SEA_PITCH, 8), BAND), :] != 0.0
        return jnp.where(inside, control_ref[j], 0.0)

    def spot(j):
        return pl.ds(pl.multiple_of(j * ROW_PITCH + step * BAND, 8), BAND)

    def advance(p, carried, add_east, add_west):
        east, west = carried
        j, k = 2 * p, SECTOR - 1 - 2 * p
        x0, x1 = taken(j), taken(j + 1)
        z0, z1 = taken(k), taken(k - 1)
        mid = keep * x0 + x1
        e0 = keep * east + x0
        e1 = keep2 * east + mid
        if add_east:
            columns[spot(j)] = columns[spot(j)] + e0
            columns[spot(j + 1)] = columns[spot(j + 1)] + e1
        else:
            columns[spot(j)] = e0
            columns[spot(j + 1)] = e1
        w0 = keep * west
        w1 = keep2 * west + keep * z0
        if add_west:
            columns[spot(k)] = columns[spot(k)] + w0
            columns[spot(k - 1)] = columns[spot(k - 1)] + w1
        else:
            columns[spot(k)] = w0
            columns[spot(k - 1)] = w1
        return e1, keep2 * west + (keep * z0 + z1)

    nothing = jnp.zeros((BAND, LANES), F32)
    pairs = SECTOR // 2
    carried = lax.fori_loop(
        0, pairs // 2 - 1, lambda p, c: advance(p, c, False, False), (nothing, nothing), unroll=3
    )
    carried = advance(pairs // 2 - 1, carried, False, False)
    carried = advance(pairs // 2, carried, False, True)
    carried = lax.fori_loop(
        pairs // 2 + 1, pairs - 1, lambda p, c: advance(p, c, True, True), carried, unroll=3
    )
    east, west = advance(pairs - 1, carried, True, True)
    columns[spot(SECTOR)] = keep * east
    columns[spot(SECTOR + 1)] = keep * west

    @pl.when(step == 0)
    def _():
        rim[0] = weight_ref[0].astype(F32)
        pl.semaphore_wait(barrier, LON + LAT - 2)
        each(LAT, lambda k: rate_copy(lat_peer(k), lat).start())
        others[lat] = constants[...]
        rim_copy(0).start()

    for half in range(BAND // 8):
        for side, value in enumerate((east, west)):
            ew[step, 2 * half + side] = value[half * 8 : half * 8 + 8]
    each(LON, lambda k: closing_copy(step, lon_peer(k), lon).start())
    gathered[step, lon] = ew[step]

    @pl.when(step == BANDS - 1)
    def _():
        rim[1] = weight_ref[BAND - 1].astype(F32)
        edge_copy(0).start()
        edge_copy(1).start()
        rim_copy(1).start()

    special = lax.broadcasted_iota(jnp.int32, (8, LANES), 0) == 7

    def forward_band(band, _):
        each(LON, lambda k: closing_copy(band, lon_peer(k), lon_peer(k)).wait_recv())
        for half in range(BAND // 8):
            q = laps[pl.ds(pl.multiple_of(band * BAND + half * 8, 8), 8)]
            whole = q
            for _ in range(4):
                whole = whole * whole
            part_of = 1.0 / (1.0 - whole)

            def gather(k, carried):
                a, b = carried
                a = q * a + gathered[band, lon_peer(k), 2 * half]
                b = q * b + gathered[band, lon_peer(LON - k), 2 * half + 1]
                return a, b

            a, b = lax.fori_loop(0, LON, gather, (zero, zero), unroll=4)
            ab[2 * half] = a * part_of
            ab[2 * half + 1] = b * part_of

        def strip(index, _):
            final = special & (jnp.full((8, LANES), index) == SHARES - 1)
            base = pl.multiple_of(index * SHARE, 8)

            def one_row(ii, north):
                row = band * BAND + ii
                entry = class_ref[row]
                keep = 1.0 - rate_ref[entry]
                gain, stride8, far = [
                    jnp.broadcast_to(rates[n, pl.ds(entry, 1), :], (8, LANES)) for n in range(3)
                ]
                at = ii // 8 * 2
                a = jnp.broadcast_to(ab[at, pl.ds(row % 8, 1), :], (8, LANES))
                b = jnp.broadcast_to(ab[at + 1, pl.ds(row % 8, 1), :], (8, LANES))
                ahead = [a * starts[index, entry, 0]]
                behind = [b * starts[index, entry, 1]]
                for _ in range(TILES - 1):
                    ahead.append(ahead[-1] * stride8)
                    behind.append(behind[-1] * stride8)
                behind = behind[::-1]
                ahead[3] = jnp.where(final, a, ahead[3])
                behind[3] = jnp.where(final, b * far, behind[3])
                done = []
                for t in range(TILES):
                    y = columns[pl.ds((base + t * 8) * ROW_PITCH + row, 8, stride=ROW_PITCH), :]
                    done.append(keep * north[t] + gain * (y + ahead[t] + behind[t]))
                    field[row, pl.ds(base + t * 8, 8), :] = done[t]
                return tuple(done)

            north = tuple(state[pl.ds(base + t * 8, 8), :] for t in range(TILES))
            north = lax.fori_loop(0, BAND, one_row, north, unroll=4)
            for t in range(TILES):
                state[pl.ds(base + t * 8, 8), :] = north[t]
            return 0

        lax.fori_loop(0, SHARES, strip, 0)
        return 0

    @pl.when(step == BANDS - 1)
    def _():
        lax.fori_loop(0, BANDS, forward_band, 0)
        closing[0] = state[...]
        each(LAT, lambda k: rate_copy(lat_peer(k), lat_peer(k)).wait_recv())

        def strip(turn, _):
            index = lax.rem(lat + turn, SHARES)
            base = pl.multiple_of(index * SHARE, 8)

            def one_row(k, south):
                row = ROWS - 1 - k
                decay = rate_ref[class_ref[row]]
                keep = 1.0 - decay
                done = []
                for t in range(TILES):
                    at = pl.ds(base + t * 8, 8)
                    done.append(keep * south[t] + decay * field[row, at, :])
                    field[row, at, :] = done[t]
                return tuple(done)

            south = lax.fori_loop(0, ROWS, one_row, (zero,) * TILES, unroll=4)
            for t in range(TILES):
                closing[1, pl.ds(base + t * 8, 8), :] = south[t]
            out_copy(index).start()

            @pl.when(index != lat)
            def _():
                share_copy(index, lat).start()

            @pl.when(index == lat)
            def _():
                lat_first[lat] = closing[:, part(lat)]

            @pl.when((lat < SHARES) & (turn == SHARES - 1))
            def _():
                each(LAT, lambda k: share_arrival(lat_peer(k)).wait_recv())
                blank = jnp.zeros((SHARE, LANES), F32)
                lat_second[0, 0] = blank
                for t in range(LAT - 1):
                    lat_second[t + 1, 0] = lat_first[t, 0] + others[t, 0:1, :] * lat_second[t, 0]
                lat_second[LAT - 1, 1] = blank
                for t in range(LAT - 1, 0, -1):
                    lat_second[t - 1, 1] = (
                        lat_first[t, 1]
                        + others[t, 1:2, :] * lat_second[t, 0]
                        + others[t, 0:1, :] * lat_second[t, 1]
                    )
                each(LAT, lambda k: reply_copy(lat_peer(k), lat).start())
                inflow_in[:, part(lat)] = lat_second[lat]

            return 0

        lax.fori_loop(0, SHARES, strip, 0)
        edge_copy(0).wait()
        edge_copy(1).wait()
        rim_copy(0).wait()
        rim_copy(1).wait()
        edges_ref[...] = edges_in[...]
        rims_ref[...] = rims_in[...]
        below_ref[...] = others[lat_peer(LAT - 1)] * (lat > 0).astype(F32)
        for band in range(BANDS):
            each(LON, lambda k: closing_copy(band, lon_peer(k), lon).wait_send())
        each(LAT, lambda k: rate_copy(lat_peer(k), lat).wait_send())

        def settle(index, c):
            @pl.when(index != lat)
            def _():
                share_copy(index, lat).wait_send()
                reply_copy(index, index).wait_recv()

            out_copy(index).wait()
            return c

        lax.fori_loop(0, SHARES, settle, 0)

        @pl.when(lat < SHARES)
        def _():
            each(LAT, lambda k: reply_copy(lat_peer(k), lat).wait_send())

        inflow_ref[...] = inflow_in[...]


def final_kernel(
    s_ref, weight_ref, mask_ref, inflow_ref, response_ref, below_ref, rims_ref, edges_ref, balance_ref,
    increment_ref, velocity_ref, mixer, picker, padded, mixed, sea, pressure, kept, factor,
):
    step = pl.program_id(0)
    lane = lane_iota(8)

    @pl.when(step == 0)
    def _():
        padded[...] = jnp.zeros_like(padded)
        padded[:COMP, :COMP] = balance_ref[...]
        high, low = split(padded[:LANES])
        mixer[:LANES, :LANES] = high
        mixer[:LANES, LANES:] = high
        mixer[LANES:, :LANES] = low
        mixer[LANES:, LANES:] = jnp.zeros_like(low)
        high, low = split(padded[COMP - LEVELS : COMP - LEVELS + 32])
        picker[:32, :LANES] = high
        picker[:32, LANES:] = high
        picker[32:, :LANES] = low
        picker[32:, LANES:] = jnp.zeros_like(low)
        row = lax.axis_index("lat") * ROWS + lax.broadcasted_iota(jnp.int32, (ROWS, LANES), 0)
        latitude = (-70.0 + 140.0 * (row.astype(F32) + 0.5) / 512.0) * (math.pi / 180.0)
        sine = jnp.sin(latitude)
        factor[...] = 0.5 * (sine / (sine * sine + 0.01))

    def operand(field):
        high, low = split(field)
        return jnp.concatenate([high, low], axis=1)

    def pressures(both):
        product = transposed_dot(picker[...], both)
        total = product[:32] + product[32:]
        end = jnp.concatenate([total[:, 2 * LANES :], jnp.zeros((32, 3 * LANES - EXTENT), F32)], axis=1)
        return [total[:, :LANES], total[:, LANES : 2 * LANES], end]

    def rim_row(field, side, row):
        rim = rims_ref[side]
        result = pressures(operand(field * rim))
        shown = transposed_dot(identity(LANES)[:32], rim.astype(BF16))
        shown = jnp.concatenate([shown, jnp.zeros((32, 3 * LANES - EXTENT), F32)], axis=1)
        for b in range(BLOCKS):
            pressure[b, row * PRESSURE_PITCH : row * PRESSURE_PITCH + 32, :] = (
                result[b] * shown[:, b * LANES : (b + 1) * LANES]
            )

    @pl.when(step == 0)
    def _():
        north, south = inflow_ref[0, :EXTENT], inflow_ref[1, :EXTENT]
        first = s_ref[0] + response_ref[0, 0:1, :] * north + response_ref[1, 0:1, :] * south
        rim_row(below_ref[2:3, :] * first + below_ref[3:4, :] * north, 0, 0)

    @pl.when(step == ROWS // 8)
    def _():
        rim_row(inflow_ref[1, :EXTENT], 1, ROWS + 1)

    @pl.when(step < ROWS // 8)
    def _():
        rows = pl.ds(pl.multiple_of(step * 8, 8), 8)
        west, east = edges_ref[0, rows], edges_ref[1, rows]
        for level in range(LEVELS):
            for block in range(BLOCKS):
                weight = mask_ref[level, :, pl.ds(block * LANES, LANES)].astype(F32)
                if block == BLOCKS - 1:
                    weight = jnp.where(lane == TAIL, lane_of(east, level), weight)
                    weight = jnp.where(lane == TAIL + 1, lane_of(west, level), weight)
                sea[block, pl.ds(level, 8, stride=PRESSURE_PITCH), :] = weight

        def one_row(i, _):
            row = step * 8 + i
            h, p = response_ref[0, pl.ds(row, 1), :], response_ref[1, pl.ds(row, 1), :]
            tail = lax.broadcasted_iota(jnp.int32, (8, LANES), 0)
            weight = weight_ref[i].astype(F32)
            e, w = edges_ref[1, pl.ds(row, 1), :], edges_ref[0, pl.ds(row, 1), :]
            end = jnp.where(tail == 6, e, jnp.where(tail == 7, w, weight[EXTENT - 8 :]))
            weight = jnp.concatenate([weight[: EXTENT - 8], end], axis=0)
            field = s_ref[i] + h * inflow_ref[0, :EXTENT] + p * inflow_ref[1, :EXTENT]
            both = operand(field * weight)
            product = transposed_dot(both, mixer[...])
            total = (product[:, :LANES] + product[:, LANES:]) * weight
            for t in range(EXTENT // 8):
                mixed[pl.ds(t * 64 + i, 8, stride=8), :] = total[t * 8 : t * 8 + 8]
            result = pressures(both)
            at = pl.multiple_of((row + 1) * PRESSURE_PITCH, 8)
            for b in range(BLOCKS):
                pressure[b, pl.ds(at, 32), :] = (
                    result[b] * sea[b, pl.ds(pl.multiple_of(i * PRESSURE_PITCH, 8), 32), :]
                )
            return 0

        lax.fori_loop(0, 8, one_row, 0, unroll=4)

        def place(j, _):
            increment_ref[j] = mixed[pl.ds(pl.multiple_of(j * 8, 8), 8), :]
            return 0

        lax.fori_loop(0, SECTOR, place, 0, unroll=10)

    @pl.when(step > 0)
    def _():
        done = step - 1
        base = done * (8 * PRESSURE_PITCH)
        scale = factor[pl.ds(pl.multiple_of(done * 8, 8), 8)]
        for level in range(LEVELS):
            centre = []
            for block in range(BLOCKS):
                below, here, above = [
                    pressure[block, pl.ds(base + k * PRESSURE_PITCH + level, 8, stride=PRESSURE_PITCH), :]
                    for k in range(3)
                ]
                centre.append(here)
                weight = kept[level, :, pl.ds(block * LANES, LANES)].astype(F32)
                velocity_ref[0, level, :, pl.ds(block * LANES, LANES)] = (
                    -scale * (above - below) * weight
                )
            ups = [pltpu.roll(c, LANES - 1, 1) for c in centre]
            downs = [pltpu.roll(c, 1, 1) for c in centre]
            wrap = pltpu.roll(centre[2], LANES - TAIL - 1, 1)
            for block in range(BLOCKS):
                right = ups[block]
                if block < BLOCKS - 1:
                    right = jnp.where(lane == LANES - 1, ups[block + 1], right)
                left = jnp.where(lane == 0, downs[block - 1] if block else wrap, downs[block])
                weight = kept[level, :, pl.ds(block * LANES, LANES)].astype(F32)
                velocity_ref[1, level, :, pl.ds(block * LANES, LANES)] = (
                    scale * (right - left) * weight
                )

    @pl.when(step < ROWS // 8)
    def _():
        kept[...] = mask_ref[...]


def body(control, land_mask, row_class, decay_rate, balance):
    wide = BLOCKS * LANES
    params = functools.partial(pltpu.CompilerParams, vmem_limit_bytes=LIMIT)

    def like(*shape, dtype=F32):
        return jax.ShapeDtypeStruct(shape, dtype)

    columns = jnp.transpose(control, (2, 1, 0))

    dma = pltpu.SemaphoreType.DMA
    fixed2, fixed3 = (lambda g: (0, 0)), (lambda g: (0, 0, 0))
    weight, s, inflow, response, below, rims, edges = pl.pallas_call(
        analysis_kernel,
        grid=(BANDS,),
        in_specs=[
            SMEM,
            SMEM,
            pl.BlockSpec((SECTOR, BAND, LANES), lambda g: (0, g, 0)),
            pl.BlockSpec((LEVELS, BAND, wide), lambda g: (0, g, 0)),
        ],
        out_specs=[
            pl.BlockSpec((BAND, EXTENT, LANES), lambda g: (g, 0, 0)),
            pl.BlockSpec(memory_space=pl.ANY),
            pl.BlockSpec((2, PADDED, LANES), fixed3),
            pl.BlockSpec((2, ROWS, LANES), fixed3),
            pl.BlockSpec((8, LANES), fixed2),
            pl.BlockSpec((2, EXTENT, LANES), fixed3),
            pl.BlockSpec((2, ROWS, LANES), fixed3),
        ],
        out_shape=[
            like(ROWS, EXTENT, LANES, dtype=BF16),
            like(ROWS, PADDED, LANES),
            like(2, PADDED, LANES),
            like(2, ROWS, LANES),
            like(8, LANES),
            like(2, EXTENT, LANES),
            like(2, ROWS, LANES),
        ],
        scratch_shapes=[
            pltpu.VMEM((BLOCKS, BAND * PITCH, LANES), F32),
            pltpu.VMEM((EXTENT * SEA_PITCH, LANES), F32),
            pltpu.VMEM((PADDED * ROW_PITCH, LANES), F32),
            pltpu.VMEM((ROWS, PADDED, LANES), F32),
            pltpu.VMEM((PADDED, LANES), F32),
            pltpu.VMEM((2, PADDED, LANES), F32),
            pltpu.VMEM((ROWS, LANES), F32),
            pltpu.VMEM((ROWS, LANES), F32),
            pltpu.VMEM((SHARES, CLASSES, 2, 8, LANES), F32),
            pltpu.VMEM((3, CLASSES, LANES), F32),
            pltpu.VMEM((BANDS, 4, 8, LANES), F32),
            pltpu.VMEM((BANDS, LON, 4, 8, LANES), F32),
            pltpu.VMEM((4, 8, LANES), F32),
            pltpu.VMEM((2, ROWS, LANES), F32),
            pltpu.VMEM((2, ROWS, LANES), F32),
            pltpu.VMEM((2, EXTENT, LANES), F32),
            pltpu.VMEM((2, EXTENT, LANES), F32),
            pltpu.VMEM((8, LANES), F32),
            pltpu.VMEM((LAT, 8, LANES), F32),
            pltpu.VMEM((LAT, 2, SHARE, LANES), F32),
            pltpu.VMEM((LAT, 2, SHARE, LANES), F32),
            pltpu.VMEM((2, PADDED, LANES), F32),
            dma((BANDS, LON)),
            dma((BANDS, LON)),
            dma((2,)),
            dma((2,)),
            dma((2,)),
            dma((2,)),
            dma((LAT,)),
            dma((LAT,)),
            dma((LAT,)),
            dma((LAT,)),
            dma((LAT,)),
            dma((LAT,)),
            dma((SHARES,)),
        ],
        compiler_params=params(collective_id=0, has_side_effects=True),
        name="analysis",
    )(row_class, decay_rate, columns, land_mask)

    increment, velocity = pl.pallas_call(
        final_kernel,
        grid=(ROWS // 8 + 1,),
        in_specs=[
            pl.BlockSpec((8, EXTENT, LANES), lambda g: (jnp.minimum(g, 7), 0, 0)),
            pl.BlockSpec((8, EXTENT, LANES), lambda g: (jnp.minimum(g, 7), 0, 0)),
            pl.BlockSpec((LEVELS, 8, wide), lambda g: (0, jnp.minimum(g, 7), 0)),
            *[VMEM] * 6,
        ],
        out_specs=[
            pl.BlockSpec((SECTOR, 8, LANES), lambda g: (0, jnp.minimum(g, 7), 0)),
            pl.BlockSpec((2, LEVELS, 8, wide), lambda g: (0, 0, jnp.maximum(g - 1, 0), 0)),
        ],
        out_shape=[like(SECTOR, ROWS, COMP), like(2, LEVELS, ROWS, SECTOR)],
        scratch_shapes=[
            pltpu.VMEM((2 * LANES, 2 * LANES), BF16),
            pltpu.VMEM((64, 2 * LANES), BF16),
            pltpu.VMEM((LANES, LANES), F32),
            pltpu.VMEM((EXTENT * 8, LANES), F32),
            pltpu.VMEM((BLOCKS, 8 * PRESSURE_PITCH, LANES), F32),
            pltpu.VMEM((BLOCKS, (ROWS + 2) * PRESSURE_PITCH, LANES), F32),
            pltpu.VMEM((LEVELS, 8, wide), jnp.int32),
            pltpu.VMEM((ROWS, LANES), F32),
        ],
        compiler_params=params(),
        name="final",
    )(s, weight, land_mask, inflow, response, below, rims, edges, balance)
    return jnp.transpose(increment, (2, 1, 0)), velocity


def solution(mesh):
    return jax.shard_map(
        body,
        mesh=mesh,
        in_specs=(P(None, "lat", "lon"), P(None, "lat", "lon"), P("lat"), P(), P()),
        out_specs=(P(None, "lat", "lon"), P(None, None, "lat", "lon")),
        check_vma=False,
    )
```

```python
import functools
import math

import jax
import jax.numpy as jnp
from jax import lax
from jax.experimental import pallas as pl
from jax.experimental.pallas import tpu as pltpu
from jax.sharding import PartitionSpec as P

COMP = 120
LEVELS = 30
ROWS = 64
SECTOR = 270
LANES = 128
BLOCKS = 3
TAIL = SECTOR - 2 * LANES
CLASSES = 16
PITCH = 136
PRESSURE_PITCH = 40
EXTENT = 272
BAND = 16
BANDS = ROWS // BAND
ROW_PITCH = 72
SEA_PITCH = 24
SHARE = 40
TILES = SHARE // 8
SHARES = 7
PADDED = SHARES * SHARE
LON = 16
LAT = 8
MESH = pl.DeviceIdType.MESH
F32 = jnp.float32
BF16 = jnp.bfloat16
SMEM = pl.BlockSpec(memory_space=pltpu.SMEM)
VMEM = pl.BlockSpec(memory_space=pltpu.VMEM)
LIMIT = 44 * 1024 * 1024


def lane_iota(rows):
    return lax.broadcasted_iota(jnp.int32, (rows, LANES), 1)


def lane_of(value, lane):
    return jnp.broadcast_to(value[:, lane : lane + 1], value.shape)


def class_decay(rate_ref):
    row = lax.broadcasted_iota(jnp.int32, (CLASSES, LANES), 0)
    decay = jnp.zeros((CLASSES, LANES), F32)
    for entry in range(CLASSES):
        decay = jnp.where(row == entry, rate_ref[entry], decay)
    return decay


def split(value):
    high = value.astype(BF16)
    return high, (value - high.astype(F32)).astype(BF16)


def transposed_dot(left, right):
    return lax.dot_general(left, right, (((1,), (1,)), ((), ())), preferred_element_type=F32)


def identity(size):
    shape = (size, size)
    same = lax.broadcasted_iota(jnp.int32, shape, 0) == lax.broadcasted_iota(jnp.int32, shape, 1)
    return same.astype(F32).astype(BF16)


def row_keep(class_ref, rate_ref, first, rows):
    at = lax.broadcasted_iota(jnp.int32, (rows, LANES), 0)
    decay = jnp.zeros((rows, LANES), F32)
    for k in range(rows):
        decay = jnp.where(at == k, rate_ref[class_ref[first + k]], decay)
    return 1.0 - decay


def widened(value):
    return jnp.concatenate([value, jnp.zeros((value.shape[0], LANES - value.shape[1]), value.dtype)], axis=1)


def block_of(ref, level, rows, block):
    if block < BLOCKS - 1:
        return ref[level, rows, pl.ds(block * LANES, LANES)]
    return widened(ref[level, rows, pl.ds(block * LANES, TAIL)])


def place_block(ref, side, level, block, value):
    if block < BLOCKS - 1:
        ref[side, level, :, pl.ds(block * LANES, LANES)] = value
    else:
        ref[side, level, :, pl.ds(block * LANES, TAIL)] = value[:, :TAIL]


def analysis_kernel(
    class_ref, rate_ref, control_ref, mask_ref,
    weight_ref, s_ref, inflow_ref, response_ref, below_ref, rims_ref, edges_ref,
    flat, sea, columns, field, state, closing, keeps, laps, starts, rates,
    ew, gathered, ab, edge, edges_in, rim, rims_in, constants, others, lat_first, lat_second, inflow_in,
    ew_send, ew_sem, edge_send, edge_sem, rim_send, rim_sem,
    rate_send, rate_sem, share_send, share_sem, reply_send, reply_sem, out_sem,
):
    step = pl.program_id(0)
    lat, lon = lax.axis_index("lat"), lax.axis_index("lon")
    barrier = pltpu.get_barrier_semaphore()

    def remote(source, target, send, recv, to):
        return pltpu.make_async_remote_copy(
            src_ref=source, dst_ref=target, send_sem=send, recv_sem=recv, device_id=to, device_id_type=MESH
        )

    def lon_peer(k):
        return lax.rem(lon + k, LON)

    def lat_peer(k):
        return lax.rem(lat + k, LAT)

    def each(count, act):
        lax.fori_loop(1, count, lambda k, c: (act(k), c)[1], 0)

    def closing_copy(band, to, slot):
        return remote(ew.at[band], gathered.at[band, slot], ew_send.at[band, to], ew_sem.at[band, slot], (lat, to))

    def edge_copy(side):
        to = lon_peer(LON - 1 if side == 0 else 1)
        return remote(edge.at[side], edges_in.at[1 - side], edge_send.at[side], edge_sem.at[1 - side], (lat, to))

    def rim_copy(side):
        to = lat_peer(LAT - 1 if side == 0 else 1)
        return remote(rim.at[side], rims_in.at[1 - side], rim_send.at[side], rim_sem.at[1 - side], (to, lon))

    def rate_copy(to, slot):
        return remote(constants, others.at[slot], rate_send.at[to], rate_sem.at[slot], (to, lon))

    def part(index):
        return pl.ds(pl.multiple_of(index * SHARE, 8), SHARE)

    def share_copy(index, slot):
        return remote(
            closing.at[:, part(index)], lat_first.at[slot], share_send.at[index], share_sem.at[slot], (index, lon)
        )

    def share_arrival(slot):
        return remote(lat_first.at[slot], lat_first.at[slot], share_send.at[slot], share_sem.at[slot], (slot, lon))

    def reply_copy(to, index):
        return remote(
            lat_second.at[to], inflow_in.at[:, part(index)], reply_send.at[to], reply_sem.at[index], (to, lon)
        )

    def out_copy(index):
        return pltpu.make_async_copy(field.at[:, part(index)], s_ref.at[:, part(index)], out_sem.at[index])

    zero = jnp.zeros((8, LANES), F32)
    ones = jnp.ones((8, LANES), F32)

    @pl.when(step == 0)
    def _():
        each(LON, lambda k: pl.semaphore_signal(barrier, inc=1, device_id=(lat, lon_peer(k)), device_id_type=MESH))
        each(LAT, lambda k: pl.semaphore_signal(barrier, inc=1, device_id=(lat_peer(k), lon), device_id_type=MESH))
        flat[...] = jnp.zeros_like(flat)
        columns[EXTENT * ROW_PITCH :] = jnp.zeros(((PADDED - EXTENT) * ROW_PITCH, LANES), F32)
        state[...] = jnp.zeros_like(state)
        for block in range(ROWS // 8):
            keep = row_keep(class_ref, rate_ref, block * 8, 8)
            keeps[block * 8 : block * 8 + 8] = keep
            q = keep * keep
            q4 = q * q
            q8 = q4 * q4
            q256 = q8
            for _ in range(5):
                q256 = q256 * q256
            laps[block * 8 : block * 8 + 8] = q256 * q8 * q4 * q
        decay = class_decay(rate_ref)
        log_keep = jnp.log(1.0 - decay)
        rates[0] = decay * jnp.sqrt(decay / (2.0 - decay))
        rates[1] = jnp.exp(log_keep * 8.0)
        rates[2] = jnp.exp(log_keep * (SECTOR + 1.0))
        row = lax.broadcasted_iota(jnp.int32, (8, LANES), 0).astype(F32)
        for entry in range(CLASSES):
            log = log_keep[entry : entry + 1]
            for index in range(SHARES):
                starts[index, entry, 0] = jnp.exp(log * (row + (SHARE * index + 1.0)))
                starts[index, entry, 1] = jnp.exp(log * (SECTOR + 8.0 - SHARE * (index + 1.0) - row))

        def onward(i, unit):
            unit = jnp.broadcast_to(keeps[pl.ds(i, 1), :], (8, LANES)) * unit
            response_ref[0, pl.ds(i, 1), :] = unit[:1]
            return unit

        product = lax.fori_loop(0, ROWS, onward, ones, unroll=4)

        def back(k, carried):
            unit, inflow = carried
            i = ROWS - 1 - k
            keep = jnp.broadcast_to(keeps[pl.ds(i, 1), :], (8, LANES))
            unit = keep * unit + (1.0 - keep) * jnp.broadcast_to(response_ref[0, pl.ds(i, 1), :], (8, LANES))
            inflow = keep * inflow
            response_ref[0, pl.ds(i, 1), :] = unit[:1]
            response_ref[1, pl.ds(i, 1), :] = inflow[:1]
            return unit, inflow

        unit, _ = lax.fori_loop(0, ROWS, back, (zero, ones), unroll=4)
        at = lax.broadcasted_iota(jnp.int32, (8, LANES), 0)
        last = jnp.broadcast_to(keeps[ROWS - 1 :], (8, LANES))
        tile = jnp.where(at == 0, product, unit)
        tile = jnp.where(at == 2, last, tile)
        constants[...] = jnp.where(at == 3, 1.0 - last, tile)

    for level in range(LEVELS):
        for half in range(BAND // 8):
            for block in range(BLOCKS):
                weight = block_of(mask_ref, level, pl.ds(half * 8, 8), block).astype(F32)
                for group in range(4):
                    place = half * 8 * PITCH + group * LEVELS + level
                    flat[block, pl.ds(place, 8, stride=PITCH), :] = weight

    eye = identity(2 * LANES)
    small = eye[:16, :LANES]

    def pair(k, _):
        at = [pl.ds(pl.multiple_of((2 * k + n) * PITCH, 8), LANES) for n in range(2)]
        parts = [
            jnp.concatenate([flat[b, at[n], :] for n in range(2)], axis=0).astype(BF16)
            for b in range(BLOCKS)
        ]
        main = transposed_dot(eye, jnp.concatenate(parts[:2], axis=1))
        tail = transposed_dot(small, parts[2])
        for n in range(2):
            whole = jnp.concatenate(
                [main[:, n * LANES : (n + 1) * LANES], tail[:, n * LANES : (n + 1) * LANES]], axis=0
            )
            row = 2 * k + n
            weight_ref[row] = whole.astype(BF16)
            for t in range(EXTENT // 8):
                sea[pl.ds(t * 8 * SEA_PITCH + row, 8, stride=SEA_PITCH), :] = whole[t * 8 : t * 8 + 8]
        return 0

    lax.fori_loop(0, BAND // 2, pair, 0, unroll=8)

    here = pl.ds(pl.multiple_of(step * BAND, BAND), BAND)
    edge[0, here] = sea[:BAND]
    edge[1, here] = sea[(SECTOR - 1) * SEA_PITCH : (SECTOR - 1) * SEA_PITCH + BAND]

    keep = keeps[here]
    keep2 = keep * keep

    def taken(j):
        inside = sea[pl.ds(pl.multiple_of(j * SEA_PITCH, 8), BAND), :] != 0.0
        return jnp.where(inside, widened(control_ref[j]), 0.0)

    def spot(j):
        return pl.ds(pl.multiple_of(j * ROW_PITCH + step * BAND, 8), BAND)

    def advance(p, carried, add_east, add_west):
        east, west = carried
        j, k = 2 * p, SECTOR - 1 - 2 * p
        x0, x1 = taken(j), taken(j + 1)
        z0, z1 = taken(k), taken(k - 1)
        mid = keep * x0 + x1
        e0 = keep * east + x0
        e1 = keep2 * east + mid
        if add_east:
            columns[spot(j)] = columns[spot(j)] + e0
            columns[spot(j + 1)] = columns[spot(j + 1)] + e1
        else:
            columns[spot(j)] = e0
            columns[spot(j + 1)] = e1
        w0 = keep * west
        w1 = keep2 * west + keep * z0
        if add_west:
            columns[spot(k)] = columns[spot(k)] + w0
            columns[spot(k - 1)] = columns[spot(k - 1)] + w1
        else:
            columns[spot(k)] = w0
            columns[spot(k - 1)] = w1
        return e1, keep2 * west + (keep * z0 + z1)

    nothing = jnp.zeros((BAND, LANES), F32)
    pairs = SECTOR // 2
    carried = lax.fori_loop(
        0, pairs // 2 - 1, lambda p, c: advance(p, c, False, False), (nothing, nothing), unroll=3
    )
    carried = advance(pairs // 2 - 1, carried, False, False)
    carried = advance(pairs // 2, carried, False, True)
    carried = lax.fori_loop(
        pairs // 2 + 1, pairs - 1, lambda p, c: advance(p, c, True, True), carried, unroll=3
    )
    east, west = advance(pairs - 1, carried, True, True)
    columns[spot(SECTOR)] = keep * east
    columns[spot(SECTOR + 1)] = keep * west

    @pl.when(step == 0)
    def _():
        rim[0] = weight_ref[0].astype(F32)
        pl.semaphore_wait(barrier, LON + LAT - 2)
        each(LAT, lambda k: rate_copy(lat_peer(k), lat).start())
        others[lat] = constants[...]
        rim_copy(0).start()

    for half in range(BAND // 8):
        for side, value in enumerate((east, west)):
            ew[step, 2 * half + side] = value[half * 8 : half * 8 + 8]
    each(LON, lambda k: closing_copy(step, lon_peer(k), lon).start())
    gathered[step, lon] = ew[step]

    @pl.when(step == BANDS - 1)
    def _():
        rim[1] = weight_ref[BAND - 1].astype(F32)
        edge_copy(0).start()
        edge_copy(1).start()
        rim_copy(1).start()

    special = lax.broadcasted_iota(jnp.int32, (8, LANES), 0) == 7

    def forward_band(band, _):
        each(LON, lambda k: closing_copy(band, lon_peer(k), lon_peer(k)).wait_recv())
        for half in range(BAND // 8):
            q = laps[pl.ds(pl.multiple_of(band * BAND + half * 8, 8), 8)]
            whole = q
            for _ in range(4):
                whole = whole * whole
            part_of = 1.0 / (1.0 - whole)

            def gather(k, carried):
                a, b = carried
                a = q * a + gathered[band, lon_peer(k), 2 * half]
                b = q * b + gathered[band, lon_peer(LON - k), 2 * half + 1]
                return a, b

            a, b = lax.fori_loop(0, LON, gather, (zero, zero), unroll=4)
            ab[2 * half] = a * part_of
            ab[2 * half + 1] = b * part_of

        def strip(index, _):
            final = special & (jnp.full((8, LANES), index) == SHARES - 1)
            base = pl.multiple_of(index * SHARE, 8)

            def one_row(ii, north):
                row = band * BAND + ii
                entry = class_ref[row]
                keep = 1.0 - rate_ref[entry]
                gain, stride8, far = [
                    jnp.broadcast_to(rates[n, pl.ds(entry, 1), :], (8, LANES)) for n in range(3)
                ]
                at = ii // 8 * 2
                a = jnp.broadcast_to(ab[at, pl.ds(row % 8, 1), :], (8, LANES))
                b = jnp.broadcast_to(ab[at + 1, pl.ds(row % 8, 1), :], (8, LANES))
                ahead = [a * starts[index, entry, 0]]
                behind = [b * starts[index, entry, 1]]
                for _ in range(TILES - 1):
                    ahead.append(ahead[-1] * stride8)
                    behind.append(behind[-1] * stride8)
                behind = behind[::-1]
                ahead[3] = jnp.where(final, a, ahead[3])
                behind[3] = jnp.where(final, b * far, behind[3])
                done = []
                for t in range(TILES):
                    y = columns[pl.ds((base + t * 8) * ROW_PITCH + row, 8, stride=ROW_PITCH), :]
                    done.append(keep * north[t] + gain * (y + ahead[t] + behind[t]))
                    field[row, pl.ds(base + t * 8, 8), :] = done[t]
                return tuple(done)

            north = tuple(state[pl.ds(base + t * 8, 8), :] for t in range(TILES))
            north = lax.fori_loop(0, BAND, one_row, north, unroll=16)
            for t in range(TILES):
                state[pl.ds(base + t * 8, 8), :] = north[t]
            return 0

        lax.fori_loop(0, SHARES, strip, 0)
        return 0

    @pl.when(step == BANDS - 1)
    def _():
        lax.fori_loop(0, BANDS, forward_band, 0)
        closing[0] = state[...]
        each(LAT, lambda k: rate_copy(lat_peer(k), lat_peer(k)).wait_recv())

        def strip(turn, _):
            index = lax.rem(lat + turn, SHARES)
            base = pl.multiple_of(index * SHARE, 8)

            def one_row(k, south):
                row = ROWS - 1 - k
                decay = rate_ref[class_ref[row]]
                keep = 1.0 - decay
                done = []
                for t in range(TILES):
                    at = pl.ds(base + t * 8, 8)
                    done.append(keep * south[t] + decay * field[row, at, :])
                    field[row, at, :] = done[t]
                return tuple(done)

            south = lax.fori_loop(0, ROWS, one_row, (zero,) * TILES, unroll=4)
            for t in range(TILES):
                closing[1, pl.ds(base + t * 8, 8), :] = south[t]
            out_copy(index).start()

            @pl.when(index != lat)
            def _():
                share_copy(index, lat).start()

            @pl.when(index == lat)
            def _():
                lat_first[lat] = closing[:, part(lat)]

            @pl.when((lat < SHARES) & (turn == SHARES - 1))
            def _():
                each(LAT, lambda k: share_arrival(lat_peer(k)).wait_recv())
                blank = jnp.zeros((SHARE, LANES), F32)
                lat_second[0, 0] = blank
                for t in range(LAT - 1):
                    lat_second[t + 1, 0] = lat_first[t, 0] + others[t, 0:1, :] * lat_second[t, 0]
                lat_second[LAT - 1, 1] = blank
                for t in range(LAT - 1, 0, -1):
                    lat_second[t - 1, 1] = (
                        lat_first[t, 1]
                        + others[t, 1:2, :] * lat_second[t, 0]
                        + others[t, 0:1, :] * lat_second[t, 1]
                    )
                each(LAT, lambda k: reply_copy(lat_peer(k), lat).start())
                inflow_in[:, part(lat)] = lat_second[lat]

            return 0

        lax.fori_loop(0, SHARES, strip, 0)
        edge_copy(0).wait()
        edge_copy(1).wait()
        rim_copy(0).wait()
        rim_copy(1).wait()
        edges_ref[...] = edges_in[...]
        rims_ref[...] = rims_in[...]
        below_ref[...] = others[lat_peer(LAT - 1)] * (lat > 0).astype(F32)
        for band in range(BANDS):
            each(LON, lambda k: closing_copy(band, lon_peer(k), lon).wait_send())
        each(LAT, lambda k: rate_copy(lat_peer(k), lat).wait_send())

        def settle(index, c):
            @pl.when(index != lat)
            def _():
                share_copy(index, lat).wait_send()
                reply_copy(index, index).wait_recv()

            out_copy(index).wait()
            return c

        lax.fori_loop(0, SHARES, settle, 0)

        @pl.when(lat < SHARES)
        def _():
            each(LAT, lambda k: reply_copy(lat_peer(k), lat).wait_send())

        inflow_ref[...] = inflow_in[...]


def final_kernel(
    s_ref, weight_ref, mask_ref, inflow_ref, response_ref, below_ref, rims_ref, edges_ref, balance_ref,
    increment_ref, velocity_ref, mixer, picker, padded, mixed, sea, pressure, kept, factor,
):
    step = pl.program_id(0)
    lane = lane_iota(8)

    @pl.when(step == 0)
    def _():
        padded[...] = jnp.zeros_like(padded)
        padded[:COMP, :COMP] = balance_ref[...]
        high, low = split(padded[:LANES])
        mixer[:LANES, :LANES] = high
        mixer[:LANES, LANES:] = high
        mixer[LANES:, :LANES] = low
        mixer[LANES:, LANES:] = jnp.zeros_like(low)
        high, low = split(padded[COMP - LEVELS : COMP - LEVELS + 32])
        picker[:32, :LANES] = high
        picker[:32, LANES:] = high
        picker[32:, :LANES] = low
        picker[32:, LANES:] = jnp.zeros_like(low)
        row = lax.axis_index("lat") * ROWS + lax.broadcasted_iota(jnp.int32, (ROWS, LANES), 0)
        latitude = (-70.0 + 140.0 * (row.astype(F32) + 0.5) / 512.0) * (math.pi / 180.0)
        sine = jnp.sin(latitude)
        factor[...] = 0.5 * (sine / (sine * sine + 0.01))

    def operand(field):
        high, low = split(field)
        return jnp.concatenate([high, low], axis=1)

    def pressures(both):
        product = transposed_dot(picker[...], both)
        total = product[:32] + product[32:]
        end = jnp.concatenate([total[:, 2 * LANES :], jnp.zeros((32, 3 * LANES - EXTENT), F32)], axis=1)
        return [total[:, :LANES], total[:, LANES : 2 * LANES], end]

    def rim_row(field, side, row):
        rim = rims_ref[side]
        result = pressures(operand(field * rim))
        shown = transposed_dot(identity(LANES)[:32], rim.astype(BF16))
        shown = jnp.concatenate([shown, jnp.zeros((32, 3 * LANES - EXTENT), F32)], axis=1)
        for b in range(BLOCKS):
            pressure[b, row * PRESSURE_PITCH : row * PRESSURE_PITCH + 32, :] = (
                result[b] * shown[:, b * LANES : (b + 1) * LANES]
            )

    @pl.when(step == 0)
    def _():
        north, south = inflow_ref[0, :EXTENT], inflow_ref[1, :EXTENT]
        first = s_ref[0] + response_ref[0, 0:1, :] * north + response_ref[1, 0:1, :] * south
        rim_row(below_ref[2:3, :] * first + below_ref[3:4, :] * north, 0, 0)

    @pl.when(step == ROWS // 8)
    def _():
        rim_row(inflow_ref[1, :EXTENT], 1, ROWS + 1)

    @pl.when(step < ROWS // 8)
    def _():
        rows = pl.ds(pl.multiple_of(step * 8, 8), 8)
        west, east = edges_ref[0, rows], edges_ref[1, rows]
        for level in range(LEVELS):
            for block in range(BLOCKS):
                weight = block_of(mask_ref, level, pl.ds(0, 8), block).astype(F32)
                if block == BLOCKS - 1:
                    weight = jnp.where(lane == TAIL, lane_of(east, level), weight)
                    weight = jnp.where(lane == TAIL + 1, lane_of(west, level), weight)
                kept[step % 2, level, :, pl.ds(block * LANES, LANES)] = weight
                sea[block, pl.ds(level, 8, stride=PRESSURE_PITCH), :] = weight

        def one_row(i, _):
            row = step * 8 + i
            h, p = response_ref[0, pl.ds(row, 1), :], response_ref[1, pl.ds(row, 1), :]
            tail = lax.broadcasted_iota(jnp.int32, (8, LANES), 0)
            weight = weight_ref[i].astype(F32)
            e, w = edges_ref[1, pl.ds(row, 1), :], edges_ref[0, pl.ds(row, 1), :]
            end = jnp.where(tail == 6, e, jnp.where(tail == 7, w, weight[EXTENT - 8 :]))
            weight = jnp.concatenate([weight[: EXTENT - 8], end], axis=0)
            field = s_ref[i] + h * inflow_ref[0, :EXTENT] + p * inflow_ref[1, :EXTENT]
            both = operand(field * weight)
            product = transposed_dot(both, mixer[...])
            total = (product[:, :LANES] + product[:, LANES:]) * weight
            for t in range(EXTENT // 8):
                mixed[pl.ds(t * 64 + i, 8, stride=8), :] = total[t * 8 : t * 8 + 8]
            result = pressures(both)
            at = pl.multiple_of((row + 1) * PRESSURE_PITCH, 8)
            for b in range(BLOCKS):
                pressure[b, pl.ds(at, 32), :] = (
                    result[b] * sea[b, pl.ds(pl.multiple_of(i * PRESSURE_PITCH, 8), 32), :]
                )
            return 0

        lax.fori_loop(0, 8, one_row, 0, unroll=8)

        def place(j, _):
            increment_ref[j] = mixed[pl.ds(pl.multiple_of(j * 8, 8), 8), :COMP]
            return 0

        lax.fori_loop(0, SECTOR, place, 0, unroll=10)

    @pl.when(step > 0)
    def _():
        done = step - 1
        base = done * (8 * PRESSURE_PITCH)
        scale = factor[pl.ds(pl.multiple_of(done * 8, 8), 8)]
        for level in range(LEVELS):
            centre = []
            for block in range(BLOCKS):
                below, here, above = [
                    pressure[block, pl.ds(base + k * PRESSURE_PITCH + level, 8, stride=PRESSURE_PITCH), :]
                    for k in range(3)
                ]
                centre.append(here)
                weight = kept[(step + 1) % 2, level, :, pl.ds(block * LANES, LANES)]
                place_block(velocity_ref, 0, level, block, -scale * (above - below) * weight)
            ups = [pltpu.roll(c, LANES - 1, 1) for c in centre]
            downs = [pltpu.roll(c, 1, 1) for c in centre]
            wrap = pltpu.roll(centre[2], LANES - TAIL - 1, 1)
            for block in range(BLOCKS):
                right = ups[block]
                if block < BLOCKS - 1:
                    right = jnp.where(lane == LANES - 1, ups[block + 1], right)
                left = jnp.where(lane == 0, downs[block - 1] if block else wrap, downs[block])
                weight = kept[(step + 1) % 2, level, :, pl.ds(block * LANES, LANES)]
                place_block(velocity_ref, 1, level, block, scale * (right - left) * weight)


def body(control, land_mask, row_class, decay_rate, balance):
    wide = BLOCKS * LANES
    params = functools.partial(pltpu.CompilerParams, vmem_limit_bytes=LIMIT)

    def like(*shape):
        return jax.ShapeDtypeStruct(shape, F32)

    columns = jnp.transpose(control, (2, 1, 0))

    dma = pltpu.SemaphoreType.DMA
    fixed2, fixed3 = (lambda g: (0, 0)), (lambda g: (0, 0, 0))
    weight, s, inflow, response, below, rims, edges = pl.pallas_call(
        analysis_kernel,
        grid=(BANDS,),
        in_specs=[
            SMEM,
            SMEM,
            pl.BlockSpec((SECTOR, BAND, COMP), lambda g: (0, g, 0)),
            pl.BlockSpec((LEVELS, BAND, SECTOR), lambda g: (0, g, 0)),
        ],
        out_specs=[
            pl.BlockSpec((BAND, EXTENT, LANES), lambda g: (g, 0, 0)),
            pl.BlockSpec(memory_space=pl.ANY),
            pl.BlockSpec((2, PADDED, LANES), fixed3),
            pl.BlockSpec((2, ROWS, LANES), fixed3),
            pl.BlockSpec((8, LANES), fixed2),
            pl.BlockSpec((2, EXTENT, LANES), fixed3),
            pl.BlockSpec((2, ROWS, LANES), fixed3),
        ],
        out_shape=[
            pltpu.VMEM((ROWS, EXTENT, LANES), BF16),
            pltpu.VMEM((ROWS, PADDED, LANES), F32),
            pltpu.VMEM((2, PADDED, LANES), F32),
            pltpu.VMEM((2, ROWS, LANES), F32),
            pltpu.VMEM((8, LANES), F32),
            pltpu.VMEM((2, EXTENT, LANES), F32),
            pltpu.VMEM((2, ROWS, LANES), F32),
        ],
        scratch_shapes=[
            pltpu.VMEM((BLOCKS, BAND * PITCH, LANES), F32),
            pltpu.VMEM((EXTENT * SEA_PITCH, LANES), F32),
            pltpu.VMEM((PADDED * ROW_PITCH, LANES), F32),
            pltpu.VMEM((ROWS, PADDED, LANES), F32),
            pltpu.VMEM((PADDED, LANES), F32),
            pltpu.VMEM((2, PADDED, LANES), F32),
            pltpu.VMEM((ROWS, LANES), F32),
            pltpu.VMEM((ROWS, LANES), F32),
            pltpu.VMEM((SHARES, CLASSES, 2, 8, LANES), F32),
            pltpu.VMEM((3, CLASSES, LANES), F32),
            pltpu.VMEM((BANDS, 4, 8, LANES), F32),
            pltpu.VMEM((BANDS, LON, 4, 8, LANES), F32),
            pltpu.VMEM((4, 8, LANES), F32),
            pltpu.VMEM((2, ROWS, LANES), F32),
            pltpu.VMEM((2, ROWS, LANES), F32),
            pltpu.VMEM((2, EXTENT, LANES), F32),
            pltpu.VMEM((2, EXTENT, LANES), F32),
            pltpu.VMEM((8, LANES), F32),
            pltpu.VMEM((LAT, 8, LANES), F32),
            pltpu.VMEM((LAT, 2, SHARE, LANES), F32),
            pltpu.VMEM((LAT, 2, SHARE, LANES), F32),
            pltpu.VMEM((2, PADDED, LANES), F32),
            dma((BANDS, LON)),
            dma((BANDS, LON)),
            dma((2,)),
            dma((2,)),
            dma((2,)),
            dma((2,)),
            dma((LAT,)),
            dma((LAT,)),
            dma((LAT,)),
            dma((LAT,)),
            dma((LAT,)),
            dma((LAT,)),
            dma((SHARES,)),
        ],
        compiler_params=params(collective_id=0, has_side_effects=True),
        name="analysis",
    )(row_class, decay_rate, columns, land_mask)

    increment, velocity = pl.pallas_call(
        final_kernel,
        grid=(ROWS // 8 + 1,),
        in_specs=[
            pl.BlockSpec((8, EXTENT, LANES), lambda g: (jnp.minimum(g, 7), 0, 0)),
            pl.BlockSpec((8, EXTENT, LANES), lambda g: (jnp.minimum(g, 7), 0, 0)),
            pl.BlockSpec((LEVELS, 8, SECTOR), lambda g: (0, jnp.minimum(g, 7), 0)),
            *[VMEM] * 6,
        ],
        out_specs=[
            pl.BlockSpec((SECTOR, 8, COMP), lambda g: (0, jnp.minimum(g, 7), 0)),
            pl.BlockSpec((2, LEVELS, 8, SECTOR), lambda g: (0, 0, jnp.maximum(g - 1, 0), 0)),
        ],
        out_shape=[like(SECTOR, ROWS, COMP), like(2, LEVELS, ROWS, SECTOR)],
        scratch_shapes=[
            pltpu.VMEM((2 * LANES, 2 * LANES), BF16),
            pltpu.VMEM((64, 2 * LANES), BF16),
            pltpu.VMEM((LANES, LANES), F32),
            pltpu.VMEM((EXTENT * 8, LANES), F32),
            pltpu.VMEM((BLOCKS, 8 * PRESSURE_PITCH, LANES), F32),
            pltpu.VMEM((BLOCKS, (ROWS + 2) * PRESSURE_PITCH, LANES), F32),
            pltpu.VMEM((2, LEVELS, 8, wide), F32),
            pltpu.VMEM((ROWS, LANES), F32),
        ],
        compiler_params=pltpu.CompilerParams(vmem_limit_bytes=24 * 1024 * 1024),
        name="final",
    )(s, weight, land_mask, inflow, response, below, rims, edges, balance)
    return jnp.transpose(increment, (2, 1, 0)), velocity


def solution(mesh):
    return jax.shard_map(
        body,
        mesh=mesh,
        in_specs=(P(None, "lat", "lon"), P(None, "lat", "lon"), P("lat"), P(), P()),
        out_specs=(P(None, "lat", "lon"), P(None, None, "lat", "lon")),
        check_vma=False,
    )
```

```python
import functools
import math

import jax
import jax.numpy as jnp
from jax import lax
from jax.experimental import pallas as pl
from jax.experimental.pallas import tpu as pltpu
from jax.sharding import PartitionSpec as P

COMP = 120
LEVELS = 30
ROWS = 64
SECTOR = 270
LANES = 128
BLOCKS = 3
TAIL = SECTOR - 2 * LANES
CLASSES = 16
PITCH = 136
PRESSURE_PITCH = 40
EXTENT = 272
BAND = 16
BANDS = ROWS // BAND
ROW_PITCH = 72
SEA_PITCH = 24
SHARE = 40
TILES = SHARE // 8
SHARES = 7
PADDED = SHARES * SHARE
LON = 16
LAT = 8
MESH = pl.DeviceIdType.MESH
F32 = jnp.float32
BF16 = jnp.bfloat16
SMEM = pl.BlockSpec(memory_space=pltpu.SMEM)
VMEM = pl.BlockSpec(memory_space=pltpu.VMEM)
LIMIT = 44 * 1024 * 1024


def lane_iota(rows):
    return lax.broadcasted_iota(jnp.int32, (rows, LANES), 1)


def lane_of(value, lane):
    return jnp.broadcast_to(value[:, lane : lane + 1], value.shape)


def class_decay(rate_ref):
    row = lax.broadcasted_iota(jnp.int32, (CLASSES, LANES), 0)
    decay = jnp.zeros((CLASSES, LANES), F32)
    for entry in range(CLASSES):
        decay = jnp.where(row == entry, rate_ref[entry], decay)
    return decay


def split(value):
    high = value.astype(BF16)
    return high, (value - high.astype(F32)).astype(BF16)


def transposed_dot(left, right):
    return lax.dot_general(left, right, (((1,), (1,)), ((), ())), preferred_element_type=F32)


def identity(size):
    shape = (size, size)
    same = lax.broadcasted_iota(jnp.int32, shape, 0) == lax.broadcasted_iota(jnp.int32, shape, 1)
    return same.astype(F32).astype(BF16)


def row_keep(class_ref, rate_ref, first, rows):
    at = lax.broadcasted_iota(jnp.int32, (rows, LANES), 0)
    decay = jnp.zeros((rows, LANES), F32)
    for k in range(rows):
        decay = jnp.where(at == k, rate_ref[class_ref[first + k]], decay)
    return 1.0 - decay


def widened(value):
    return jnp.concatenate([value, jnp.zeros((value.shape[0], LANES - value.shape[1]), value.dtype)], axis=1)


def block_of(ref, level, rows, block):
    if block < BLOCKS - 1:
        return ref[level, rows, pl.ds(block * LANES, LANES)]
    return widened(ref[level, rows, pl.ds(block * LANES, TAIL)])


def place_block(ref, side, level, block, value):
    if block < BLOCKS - 1:
        ref[side, level, :, pl.ds(block * LANES, LANES)] = value
    else:
        ref[side, level, :, pl.ds(block * LANES, TAIL)] = value[:, :TAIL]


def analysis_kernel(
    class_ref, rate_ref, control_ref, mask_ref,
    weight_ref, s_ref, inflow_ref, response_ref, below_ref, rims_ref, edges_ref,
    flat, sea, columns, field, state, closing, keeps, laps, starts, rates,
    ew, gathered, ab, edge, edges_in, rim, rims_in, constants, others, lat_first, lat_second, inflow_in,
    ew_send, ew_sem, edge_send, edge_sem, rim_send, rim_sem,
    rate_send, rate_sem, share_send, share_sem, reply_send, reply_sem, out_sem,
):
    step = pl.program_id(0)
    lat, lon = lax.axis_index("lat"), lax.axis_index("lon")
    barrier = pltpu.get_barrier_semaphore()

    def remote(source, target, send, recv, to):
        return pltpu.make_async_remote_copy(
            src_ref=source, dst_ref=target, send_sem=send, recv_sem=recv, device_id=to, device_id_type=MESH
        )

    def lon_peer(k):
        return lax.rem(lon + k, LON)

    def lat_peer(k):
        return lax.rem(lat + k, LAT)

    def each(count, act):
        lax.fori_loop(1, count, lambda k, c: (act(k), c)[1], 0)

    def closing_copy(band, to, slot):
        return remote(ew.at[band], gathered.at[band, slot], ew_send.at[band, to], ew_sem.at[band, slot], (lat, to))

    def edge_copy(side):
        to = lon_peer(LON - 1 if side == 0 else 1)
        return remote(edge.at[side], edges_in.at[1 - side], edge_send.at[side], edge_sem.at[1 - side], (lat, to))

    def rim_copy(side):
        to = lat_peer(LAT - 1 if side == 0 else 1)
        return remote(rim.at[side], rims_in.at[1 - side], rim_send.at[side], rim_sem.at[1 - side], (to, lon))

    def rate_copy(to, slot):
        return remote(constants, others.at[slot], rate_send.at[to], rate_sem.at[slot], (to, lon))

    def part(index):
        return pl.ds(pl.multiple_of(index * SHARE, 8), SHARE)

    def share_copy(side, index, slot):
        return remote(
            closing.at[side, part(index)], lat_first.at[slot, side],
            share_send.at[side, index], share_sem.at[side, slot], (index, lon),
        )

    def share_arrival(side, slot):
        return remote(
            lat_first.at[slot, side], lat_first.at[slot, side],
            share_send.at[side, slot], share_sem.at[side, slot], (slot, lon),
        )

    def reply_copy(side, to, index):
        return remote(
            lat_second.at[to, side], inflow_in.at[side, part(index)],
            reply_send.at[side, to], reply_sem.at[side, index], (to, lon),
        )

    def far_lat(k):
        return lat_peer(lax.rem(k + 2, LAT - 1) + 1)

    def far_lon(k):
        return lon_peer(lax.rem(k + 6, LON - 1) + 1)

    def out_copy(index):
        return pltpu.make_async_copy(field.at[:, part(index)], s_ref.at[:, part(index)], out_sem.at[index])

    zero = jnp.zeros((8, LANES), F32)
    ones = jnp.ones((8, LANES), F32)

    @pl.when(step == 0)
    def _():
        each(LON, lambda k: pl.semaphore_signal(barrier, inc=1, device_id=(lat, lon_peer(k)), device_id_type=MESH))
        each(LAT, lambda k: pl.semaphore_signal(barrier, inc=1, device_id=(lat_peer(k), lon), device_id_type=MESH))
        flat[...] = jnp.zeros_like(flat)
        columns[EXTENT * ROW_PITCH :] = jnp.zeros(((PADDED - EXTENT) * ROW_PITCH, LANES), F32)
        state[...] = jnp.zeros_like(state)
        for block in range(ROWS // 8):
            keep = row_keep(class_ref, rate_ref, block * 8, 8)
            keeps[block * 8 : block * 8 + 8] = keep
            q = keep * keep
            q4 = q * q
            q8 = q4 * q4
            q256 = q8
            for _ in range(5):
                q256 = q256 * q256
            laps[block * 8 : block * 8 + 8] = q256 * q8 * q4 * q
        decay = class_decay(rate_ref)
        log_keep = jnp.log(1.0 - decay)
        rates[0] = decay * jnp.sqrt(decay / (2.0 - decay))
        rates[1] = jnp.exp(log_keep * 8.0)
        rates[2] = jnp.exp(log_keep * (SECTOR + 1.0))
        row = lax.broadcasted_iota(jnp.int32, (8, LANES), 0).astype(F32)
        for entry in range(CLASSES):
            log = log_keep[entry : entry + 1]
            for index in range(SHARES):
                starts[index, entry, 0] = jnp.exp(log * (row + (SHARE * index + 1.0)))
                starts[index, entry, 1] = jnp.exp(log * (SECTOR + 8.0 - SHARE * (index + 1.0) - row))

        def onward(i, unit):
            unit = jnp.broadcast_to(keeps[pl.ds(i, 1), :], (8, LANES)) * unit
            response_ref[0, pl.ds(i, 1), :] = unit[:1]
            return unit

        product = lax.fori_loop(0, ROWS, onward, ones, unroll=4)

        def back(k, carried):
            unit, inflow = carried
            i = ROWS - 1 - k
            keep = jnp.broadcast_to(keeps[pl.ds(i, 1), :], (8, LANES))
            unit = keep * unit + (1.0 - keep) * jnp.broadcast_to(response_ref[0, pl.ds(i, 1), :], (8, LANES))
            inflow = keep * inflow
            response_ref[0, pl.ds(i, 1), :] = unit[:1]
            response_ref[1, pl.ds(i, 1), :] = inflow[:1]
            return unit, inflow

        unit, _ = lax.fori_loop(0, ROWS, back, (zero, ones), unroll=4)
        at = lax.broadcasted_iota(jnp.int32, (8, LANES), 0)
        last = jnp.broadcast_to(keeps[ROWS - 1 :], (8, LANES))
        tile = jnp.where(at == 0, product, unit)
        tile = jnp.where(at == 2, last, tile)
        constants[...] = jnp.where(at == 3, 1.0 - last, tile)

    for level in range(LEVELS):
        for half in range(BAND // 8):
            for block in range(BLOCKS):
                weight = block_of(mask_ref, level, pl.ds(half * 8, 8), block).astype(F32)
                for group in range(4):
                    place = half * 8 * PITCH + group * LEVELS + level
                    flat[block, pl.ds(place, 8, stride=PITCH), :] = weight

    eye = identity(2 * LANES)
    small = eye[:16, :LANES]

    def pair(k, _):
        at = [pl.ds(pl.multiple_of((2 * k + n) * PITCH, 8), LANES) for n in range(2)]
        parts = [
            jnp.concatenate([flat[b, at[n], :] for n in range(2)], axis=0).astype(BF16)
            for b in range(BLOCKS)
        ]
        main = transposed_dot(eye, jnp.concatenate(parts[:2], axis=1))
        tail = transposed_dot(small, parts[2])
        for n in range(2):
            whole = jnp.concatenate(
                [main[:, n * LANES : (n + 1) * LANES], tail[:, n * LANES : (n + 1) * LANES]], axis=0
            )
            row = 2 * k + n
            weight_ref[row] = whole.astype(BF16)
            for t in range(EXTENT // 8):
                sea[pl.ds(t * 8 * SEA_PITCH + row, 8, stride=SEA_PITCH), :] = whole[t * 8 : t * 8 + 8]
        return 0

    lax.fori_loop(0, BAND // 2, pair, 0, unroll=8)

    here = pl.ds(pl.multiple_of(step * BAND, BAND), BAND)
    edge[0, here] = sea[:BAND]
    edge[1, here] = sea[(SECTOR - 1) * SEA_PITCH : (SECTOR - 1) * SEA_PITCH + BAND]

    keep = keeps[here]
    keep2 = keep * keep

    def taken(j):
        inside = sea[pl.ds(pl.multiple_of(j * SEA_PITCH, 8), BAND), :] != 0.0
        return jnp.where(inside, widened(control_ref[j]), 0.0)

    def spot(j):
        return pl.ds(pl.multiple_of(j * ROW_PITCH + step * BAND, 8), BAND)

    def advance(p, carried, add_east, add_west):
        east, west = carried
        j, k = 2 * p, SECTOR - 1 - 2 * p
        x0, x1 = taken(j), taken(j + 1)
        z0, z1 = taken(k), taken(k - 1)
        mid = keep * x0 + x1
        e0 = keep * east + x0
        e1 = keep2 * east + mid
        if add_east:
            columns[spot(j)] = columns[spot(j)] + e0
            columns[spot(j + 1)] = columns[spot(j + 1)] + e1
        else:
            columns[spot(j)] = e0
            columns[spot(j + 1)] = e1
        w0 = keep * west
        w1 = keep2 * west + keep * z0
        if add_west:
            columns[spot(k)] = columns[spot(k)] + w0
            columns[spot(k - 1)] = columns[spot(k - 1)] + w1
        else:
            columns[spot(k)] = w0
            columns[spot(k - 1)] = w1
        return e1, keep2 * west + (keep * z0 + z1)

    nothing = jnp.zeros((BAND, LANES), F32)
    pairs = SECTOR // 2
    carried = lax.fori_loop(
        0, pairs // 2 - 1, lambda p, c: advance(p, c, False, False), (nothing, nothing), unroll=3
    )
    carried = advance(pairs // 2 - 1, carried, False, False)
    carried = advance(pairs // 2, carried, False, True)
    carried = lax.fori_loop(
        pairs // 2 + 1, pairs - 1, lambda p, c: advance(p, c, True, True), carried, unroll=3
    )
    east, west = advance(pairs - 1, carried, True, True)
    columns[spot(SECTOR)] = keep * east
    columns[spot(SECTOR + 1)] = keep * west

    @pl.when(step == 0)
    def _():
        rim[0] = weight_ref[0].astype(F32)
        pl.semaphore_wait(barrier, LON + LAT - 2)
        each(LAT, lambda k: rate_copy(lat_peer(k), lat).start())
        others[lat] = constants[...]
        rim_copy(0).start()

    for half in range(BAND // 8):
        for side, value in enumerate((east, west)):
            ew[step, 2 * half + side] = value[half * 8 : half * 8 + 8]
    each(LON, lambda k: closing_copy(step, far_lon(k), lon).start())
    gathered[step, lon] = ew[step]

    @pl.when(step == BANDS - 1)
    def _():
        rim[1] = weight_ref[BAND - 1].astype(F32)
        edge_copy(0).start()
        edge_copy(1).start()
        rim_copy(1).start()

    special = lax.broadcasted_iota(jnp.int32, (8, LANES), 0) == 7

    def forward_band(band, _):
        each(LON, lambda k: closing_copy(band, lon_peer(k), lon_peer(k)).wait_recv())
        for half in range(BAND // 8):
            q = laps[pl.ds(pl.multiple_of(band * BAND + half * 8, 8), 8)]
            whole = q
            for _ in range(4):
                whole = whole * whole
            part_of = 1.0 / (1.0 - whole)

            def gather(k, carried):
                a, b = carried
                a = q * a + gathered[band, lon_peer(k), 2 * half]
                b = q * b + gathered[band, lon_peer(LON - k), 2 * half + 1]
                return a, b

            a, b = lax.fori_loop(0, LON, gather, (zero, zero), unroll=4)
            ab[2 * half] = a * part_of
            ab[2 * half + 1] = b * part_of

        def strip(index, _):
            final = special & (jnp.full((8, LANES), index) == SHARES - 1)
            base = pl.multiple_of(index * SHARE, 8)

            def one_row(ii, north):
                row = band * BAND + ii
                entry = class_ref[row]
                keep = 1.0 - rate_ref[entry]
                gain, stride8, far = [
                    jnp.broadcast_to(rates[n, pl.ds(entry, 1), :], (8, LANES)) for n in range(3)
                ]
                at = ii // 8 * 2
                a = jnp.broadcast_to(ab[at, pl.ds(row % 8, 1), :], (8, LANES))
                b = jnp.broadcast_to(ab[at + 1, pl.ds(row % 8, 1), :], (8, LANES))
                ahead = [a * starts[index, entry, 0]]
                behind = [b * starts[index, entry, 1]]
                for _ in range(TILES - 1):
                    ahead.append(ahead[-1] * stride8)
                    behind.append(behind[-1] * stride8)
                behind = behind[::-1]
                ahead[3] = jnp.where(final, a, ahead[3])
                behind[3] = jnp.where(final, b * far, behind[3])
                done = []
                for t in range(TILES):
                    y = columns[pl.ds((base + t * 8) * ROW_PITCH + row, 8, stride=ROW_PITCH), :]
                    done.append(keep * north[t] + gain * (y + ahead[t] + behind[t]))
                    field[row, pl.ds(base + t * 8, 8), :] = done[t]
                return tuple(done)

            north = tuple(state[pl.ds(base + t * 8, 8), :] for t in range(TILES))
            north = lax.fori_loop(0, BAND, one_row, north, unroll=16)
            for t in range(TILES):
                state[pl.ds(base + t * 8, 8), :] = north[t]
            return 0

        lax.fori_loop(0, SHARES, strip, 0)
        return 0

    @pl.when(step == BANDS - 1)
    def _():
        lax.fori_loop(0, BANDS, forward_band, 0)
        closing[0] = state[...]

        def send_north(k, c):
            index = lax.rem(lat + 1 + k, SHARES)

            @pl.when(index != lat)
            def _():
                share_copy(0, index, lat).start()

            @pl.when(index == lat)
            def _():
                lat_first[lat, 0] = closing[0, part(lat)]

            return c

        lax.fori_loop(0, SHARES, send_north, 0)
        each(LAT, lambda k: rate_copy(lat_peer(k), lat_peer(k)).wait_recv())

        def strip(turn, _):
            index = lax.rem(lat + 1 + turn, SHARES)
            base = pl.multiple_of(index * SHARE, 8)

            def one_row(k, south):
                row = ROWS - 1 - k
                decay = rate_ref[class_ref[row]]
                keep = 1.0 - decay
                done = []
                for t in range(TILES):
                    at = pl.ds(base + t * 8, 8)
                    done.append(keep * south[t] + decay * field[row, at, :])
                    field[row, at, :] = done[t]
                return tuple(done)

            south = lax.fori_loop(0, ROWS, one_row, (zero,) * TILES, unroll=4)
            for t in range(TILES):
                closing[1, pl.ds(base + t * 8, 8), :] = south[t]
            out_copy(index).start()

            @pl.when(index != lat)
            def _():
                share_copy(1, index, lat).start()

            @pl.when(index == lat)
            def _():
                lat_first[lat, 1] = closing[1, part(lat)]

            @pl.when((lat < SHARES) & (turn == SHARES - 2))
            def _():
                each(LAT, lambda k: share_arrival(0, lat_peer(k)).wait_recv())
                lat_second[0, 0] = jnp.zeros((SHARE, LANES), F32)
                for t in range(LAT - 1):
                    lat_second[t + 1, 0] = lat_first[t, 0] + others[t, 0:1, :] * lat_second[t, 0]
                each(LAT, lambda k: reply_copy(0, far_lat(k), lat).start())
                inflow_in[0, part(lat)] = lat_second[lat, 0]

            @pl.when((lat < SHARES) & (turn == SHARES - 1))
            def _():
                each(LAT, lambda k: share_arrival(1, lat_peer(k)).wait_recv())
                lat_second[LAT - 1, 1] = jnp.zeros((SHARE, LANES), F32)
                for t in range(LAT - 1, 0, -1):
                    lat_second[t - 1, 1] = (
                        lat_first[t, 1]
                        + others[t, 1:2, :] * lat_second[t, 0]
                        + others[t, 0:1, :] * lat_second[t, 1]
                    )
                each(LAT, lambda k: reply_copy(1, far_lat(k), lat).start())
                inflow_in[1, part(lat)] = lat_second[lat, 1]

            return 0

        lax.fori_loop(0, SHARES, strip, 0)
        edge_copy(0).wait()
        edge_copy(1).wait()
        rim_copy(0).wait()
        rim_copy(1).wait()
        edges_ref[...] = edges_in[...]
        rims_ref[...] = rims_in[...]
        below_ref[...] = others[lat_peer(LAT - 1)] * (lat > 0).astype(F32)
        for band in range(BANDS):
            each(LON, lambda k: closing_copy(band, lon_peer(k), lon).wait_send())
        each(LAT, lambda k: rate_copy(lat_peer(k), lat).wait_send())

        def settle(index, c):
            @pl.when(index != lat)
            def _():
                for side in range(2):
                    share_copy(side, index, lat).wait_send()
                    reply_copy(side, index, index).wait_recv()

            out_copy(index).wait()
            return c

        lax.fori_loop(0, SHARES, settle, 0)

        @pl.when(lat < SHARES)
        def _():
            for side in range(2):
                each(LAT, lambda k: reply_copy(side, lat_peer(k), lat).wait_send())

        inflow_ref[...] = inflow_in[...]


def final_kernel(
    s_ref, weight_ref, mask_ref, inflow_ref, response_ref, below_ref, rims_ref, edges_ref, balance_ref,
    increment_ref, velocity_ref, mixer, picker, padded, mixed, sea, pressure, kept, factor,
):
    step = pl.program_id(0)
    lane = lane_iota(8)

    @pl.when(step == 0)
    def _():
        padded[...] = jnp.zeros_like(padded)
        padded[:COMP, :COMP] = balance_ref[...]
        high, low = split(padded[:LANES])
        mixer[:LANES, :LANES] = high
        mixer[:LANES, LANES:] = high
        mixer[LANES:, :LANES] = low
        mixer[LANES:, LANES:] = jnp.zeros_like(low)
        high, low = split(padded[COMP - LEVELS : COMP - LEVELS + 32])
        picker[:32, :LANES] = high
        picker[:32, LANES:] = high
        picker[32:, :LANES] = low
        picker[32:, LANES:] = jnp.zeros_like(low)
        row = lax.axis_index("lat") * ROWS + lax.broadcasted_iota(jnp.int32, (ROWS, LANES), 0)
        latitude = (-70.0 + 140.0 * (row.astype(F32) + 0.5) / 512.0) * (math.pi / 180.0)
        sine = jnp.sin(latitude)
        factor[...] = 0.5 * (sine / (sine * sine + 0.01))

    def operand(field):
        high, low = split(field)
        return jnp.concatenate([high, low], axis=1)

    def pressures(both):
        product = transposed_dot(picker[...], both)
        total = product[:32] + product[32:]
        end = jnp.concatenate([total[:, 2 * LANES :], jnp.zeros((32, 3 * LANES - EXTENT), F32)], axis=1)
        return [total[:, :LANES], total[:, LANES : 2 * LANES], end]

    def rim_row(field, side, row):
        rim = rims_ref[side]
        result = pressures(operand(field * rim))
        shown = transposed_dot(identity(LANES)[:32], rim.astype(BF16))
        shown = jnp.concatenate([shown, jnp.zeros((32, 3 * LANES - EXTENT), F32)], axis=1)
        for b in range(BLOCKS):
            pressure[b, row * PRESSURE_PITCH : row * PRESSURE_PITCH + 32, :] = (
                result[b] * shown[:, b * LANES : (b + 1) * LANES]
            )

    @pl.when(step == 0)
    def _():
        north, south = inflow_ref[0, :EXTENT], inflow_ref[1, :EXTENT]
        first = s_ref[0] + response_ref[0, 0:1, :] * north + response_ref[1, 0:1, :] * south
        rim_row(below_ref[2:3, :] * first + below_ref[3:4, :] * north, 0, 0)

    @pl.when(step == ROWS // 8)
    def _():
        rim_row(inflow_ref[1, :EXTENT], 1, ROWS + 1)

    @pl.when(step < ROWS // 8)
    def _():
        rows = pl.ds(pl.multiple_of(step * 8, 8), 8)
        west, east = edges_ref[0, rows], edges_ref[1, rows]
        for level in range(LEVELS):
            for block in range(BLOCKS):
                weight = block_of(mask_ref, level, pl.ds(0, 8), block).astype(F32)
                if block == BLOCKS - 1:
                    weight = jnp.where(lane == TAIL, lane_of(east, level), weight)
                    weight = jnp.where(lane == TAIL + 1, lane_of(west, level), weight)
                kept[step % 2, level, :, pl.ds(block * LANES, LANES)] = weight
                sea[block, pl.ds(level, 8, stride=PRESSURE_PITCH), :] = weight

        def one_row(i, _):
            row = step * 8 + i
            h, p = response_ref[0, pl.ds(row, 1), :], response_ref[1, pl.ds(row, 1), :]
            tail = lax.broadcasted_iota(jnp.int32, (8, LANES), 0)
            weight = weight_ref[i].astype(F32)
            e, w = edges_ref[1, pl.ds(row, 1), :], edges_ref[0, pl.ds(row, 1), :]
            end = jnp.where(tail == 6, e, jnp.where(tail == 7, w, weight[EXTENT - 8 :]))
            weight = jnp.concatenate([weight[: EXTENT - 8], end], axis=0)
            field = s_ref[i] + h * inflow_ref[0, :EXTENT] + p * inflow_ref[1, :EXTENT]
            both = operand(field * weight)
            product = transposed_dot(both, mixer[...])
            total = (product[:, :LANES] + product[:, LANES:]) * weight
            for t in range(EXTENT // 8):
                mixed[pl.ds(t * 64 + i, 8, stride=8), :] = total[t * 8 : t * 8 + 8]
            result = pressures(both)
            at = pl.multiple_of((row + 1) * PRESSURE_PITCH, 8)
            for b in range(BLOCKS):
                pressure[b, pl.ds(at, 32), :] = (
                    result[b] * sea[b, pl.ds(pl.multiple_of(i * PRESSURE_PITCH, 8), 32), :]
                )
            return 0

        lax.fori_loop(0, 8, one_row, 0, unroll=8)

        def place(j, _):
            increment_ref[j] = mixed[pl.ds(pl.multiple_of(j * 8, 8), 8), :COMP]
            return 0

        lax.fori_loop(0, SECTOR, place, 0, unroll=10)

    @pl.when(step > 0)
    def _():
        done = step - 1
        base = done * (8 * PRESSURE_PITCH)
        scale = factor[pl.ds(pl.multiple_of(done * 8, 8), 8)]
        for level in range(LEVELS):
            centre = []
            for block in range(BLOCKS):
                below, here, above = [
                    pressure[block, pl.ds(base + k * PRESSURE_PITCH + level, 8, stride=PRESSURE_PITCH), :]
                    for k in range(3)
                ]
                centre.append(here)
                weight = kept[(step + 1) % 2, level, :, pl.ds(block * LANES, LANES)]
                place_block(velocity_ref, 0, level, block, -scale * (above - below) * weight)
            ups = [pltpu.roll(c, LANES - 1, 1) for c in centre]
            downs = [pltpu.roll(c, 1, 1) for c in centre]
            wrap = pltpu.roll(centre[2], LANES - TAIL - 1, 1)
            for block in range(BLOCKS):
                right = ups[block]
                if block < BLOCKS - 1:
                    right = jnp.where(lane == LANES - 1, ups[block + 1], right)
                left = jnp.where(lane == 0, downs[block - 1] if block else wrap, downs[block])
                weight = kept[(step + 1) % 2, level, :, pl.ds(block * LANES, LANES)]
                place_block(velocity_ref, 1, level, block, scale * (right - left) * weight)


def body(control, land_mask, row_class, decay_rate, balance):
    wide = BLOCKS * LANES
    params = functools.partial(pltpu.CompilerParams, vmem_limit_bytes=LIMIT)

    def like(*shape):
        return jax.ShapeDtypeStruct(shape, F32)

    columns = jnp.transpose(control, (2, 1, 0))

    dma = pltpu.SemaphoreType.DMA
    fixed2, fixed3 = (lambda g: (0, 0)), (lambda g: (0, 0, 0))
    weight, s, inflow, response, below, rims, edges = pl.pallas_call(
        analysis_kernel,
        grid=(BANDS,),
        in_specs=[
            SMEM,
            SMEM,
            pl.BlockSpec((SECTOR, BAND, COMP), lambda g: (0, g, 0)),
            pl.BlockSpec((LEVELS, BAND, SECTOR), lambda g: (0, g, 0)),
        ],
        out_specs=[
            pl.BlockSpec((BAND, EXTENT, LANES), lambda g: (g, 0, 0)),
            pl.BlockSpec(memory_space=pl.ANY),
            pl.BlockSpec((2, PADDED, LANES), fixed3),
            pl.BlockSpec((2, ROWS, LANES), fixed3),
            pl.BlockSpec((8, LANES), fixed2),
            pl.BlockSpec((2, EXTENT, LANES), fixed3),
            pl.BlockSpec((2, ROWS, LANES), fixed3),
        ],
        out_shape=[
            pltpu.VMEM((ROWS, EXTENT, LANES), BF16),
            pltpu.VMEM((ROWS, PADDED, LANES), F32),
            pltpu.VMEM((2, PADDED, LANES), F32),
            pltpu.VMEM((2, ROWS, LANES), F32),
            pltpu.VMEM((8, LANES), F32),
            pltpu.VMEM((2, EXTENT, LANES), F32),
            pltpu.VMEM((2, ROWS, LANES), F32),
        ],
        scratch_shapes=[
            pltpu.VMEM((BLOCKS, BAND * PITCH, LANES), F32),
            pltpu.VMEM((EXTENT * SEA_PITCH, LANES), F32),
            pltpu.VMEM((PADDED * ROW_PITCH, LANES), F32),
            pltpu.VMEM((ROWS, PADDED, LANES), F32),
            pltpu.VMEM((PADDED, LANES), F32),
            pltpu.VMEM((2, PADDED, LANES), F32),
            pltpu.VMEM((ROWS, LANES), F32),
            pltpu.VMEM((ROWS, LANES), F32),
            pltpu.VMEM((SHARES, CLASSES, 2, 8, LANES), F32),
            pltpu.VMEM((3, CLASSES, LANES), F32),
            pltpu.VMEM((BANDS, 4, 8, LANES), F32),
            pltpu.VMEM((BANDS, LON, 4, 8, LANES), F32),
            pltpu.VMEM((4, 8, LANES), F32),
            pltpu.VMEM((2, ROWS, LANES), F32),
            pltpu.VMEM((2, ROWS, LANES), F32),
            pltpu.VMEM((2, EXTENT, LANES), F32),
            pltpu.VMEM((2, EXTENT, LANES), F32),
            pltpu.VMEM((8, LANES), F32),
            pltpu.VMEM((LAT, 8, LANES), F32),
            pltpu.VMEM((LAT, 2, SHARE, LANES), F32),
            pltpu.VMEM((LAT, 2, SHARE, LANES), F32),
            pltpu.VMEM((2, PADDED, LANES), F32),
            dma((BANDS, LON)),
            dma((BANDS, LON)),
            dma((2,)),
            dma((2,)),
            dma((2,)),
            dma((2,)),
            dma((LAT,)),
            dma((LAT,)),
            dma((2, LAT)),
            dma((2, LAT)),
            dma((2, LAT)),
            dma((2, LAT)),
            dma((SHARES,)),
        ],
        compiler_params=params(collective_id=0, has_side_effects=True),
        name="analysis",
    )(row_class, decay_rate, columns, land_mask)

    increment, velocity = pl.pallas_call(
        final_kernel,
        grid=(ROWS // 8 + 1,),
        in_specs=[
            pl.BlockSpec((8, EXTENT, LANES), lambda g: (jnp.minimum(g, 7), 0, 0)),
            pl.BlockSpec((8, EXTENT, LANES), lambda g: (jnp.minimum(g, 7), 0, 0)),
            pl.BlockSpec((LEVELS, 8, SECTOR), lambda g: (0, jnp.minimum(g, 7), 0)),
            *[VMEM] * 6,
        ],
        out_specs=[
            pl.BlockSpec((SECTOR, 8, COMP), lambda g: (0, jnp.minimum(g, 7), 0)),
            pl.BlockSpec((2, LEVELS, 8, SECTOR), lambda g: (0, 0, jnp.maximum(g - 1, 0), 0)),
        ],
        out_shape=[like(SECTOR, ROWS, COMP), like(2, LEVELS, ROWS, SECTOR)],
        scratch_shapes=[
            pltpu.VMEM((2 * LANES, 2 * LANES), BF16),
            pltpu.VMEM((64, 2 * LANES), BF16),
            pltpu.VMEM((LANES, LANES), F32),
            pltpu.VMEM((EXTENT * 8, LANES), F32),
            pltpu.VMEM((BLOCKS, 8 * PRESSURE_PITCH, LANES), F32),
            pltpu.VMEM((BLOCKS, (ROWS + 2) * PRESSURE_PITCH, LANES), F32),
            pltpu.VMEM((2, LEVELS, 8, wide), F32),
            pltpu.VMEM((ROWS, LANES), F32),
        ],
        compiler_params=pltpu.CompilerParams(vmem_limit_bytes=24 * 1024 * 1024),
        name="final",
    )(s, weight, land_mask, inflow, response, below, rims, edges, balance)
    return jnp.transpose(increment, (2, 1, 0)), velocity


def solution(mesh):
    return jax.shard_map(
        body,
        mesh=mesh,
        in_specs=(P(None, "lat", "lon"), P(None, "lat", "lon"), P("lat"), P(), P()),
        out_specs=(P(None, "lat", "lon"), P(None, None, "lat", "lon")),
        check_vma=False,
    )
```

```python
import functools
import math

import jax
import jax.numpy as jnp
from jax import lax
from jax.experimental import pallas as pl
from jax.experimental.pallas import tpu as pltpu
from jax.sharding import PartitionSpec as P

COMP = 120
LEVELS = 30
ROWS = 64
SECTOR = 270
LANES = 128
BLOCKS = 3
TAIL = SECTOR - 2 * LANES
CLASSES = 16
PITCH = 136
PRESSURE_PITCH = 40
EXTENT = 272
BAND = 16
BANDS = ROWS // BAND
ROW_PITCH = 72
SEA_PITCH = 24
SHARE = 40
TILES = SHARE // 8
SHARES = 7
PADDED = SHARES * SHARE
LON = 16
LAT = 8
MESH = pl.DeviceIdType.MESH
F32 = jnp.float32
BF16 = jnp.bfloat16
SMEM = pl.BlockSpec(memory_space=pltpu.SMEM)
VMEM = pl.BlockSpec(memory_space=pltpu.VMEM)
LIMIT = 44 * 1024 * 1024


def lane_iota(rows):
    return lax.broadcasted_iota(jnp.int32, (rows, LANES), 1)


def lane_of(value, lane):
    return jnp.broadcast_to(value[:, lane : lane + 1], value.shape)


def class_decay(rate_ref):
    row = lax.broadcasted_iota(jnp.int32, (CLASSES, LANES), 0)
    decay = jnp.zeros((CLASSES, LANES), F32)
    for entry in range(CLASSES):
        decay = jnp.where(row == entry, rate_ref[entry], decay)
    return decay


def split(value):
    high = value.astype(BF16)
    return high, (value - high.astype(F32)).astype(BF16)


def transposed_dot(left, right):
    return lax.dot_general(left, right, (((1,), (1,)), ((), ())), preferred_element_type=F32)


def identity(size):
    shape = (size, size)
    same = lax.broadcasted_iota(jnp.int32, shape, 0) == lax.broadcasted_iota(jnp.int32, shape, 1)
    return same.astype(F32).astype(BF16)


def row_keep(class_ref, rate_ref, first, rows):
    at = lax.broadcasted_iota(jnp.int32, (rows, LANES), 0)
    decay = jnp.zeros((rows, LANES), F32)
    for k in range(rows):
        decay = jnp.where(at == k, rate_ref[class_ref[first + k]], decay)
    return 1.0 - decay


def widened(value):
    return jnp.concatenate([value, jnp.zeros((value.shape[0], LANES - value.shape[1]), value.dtype)], axis=1)


def block_of(ref, level, rows, block):
    if block < BLOCKS - 1:
        return ref[level, rows, pl.ds(block * LANES, LANES)]
    return widened(ref[level, rows, pl.ds(block * LANES, TAIL)])


def place_block(ref, side, level, block, value):
    if block < BLOCKS - 1:
        ref[side, level, :, pl.ds(block * LANES, LANES)] = value
    else:
        ref[side, level, :, pl.ds(block * LANES, TAIL)] = value[:, :TAIL]


def analysis_kernel(
    class_ref, rate_ref, control_ref, mask_ref,
    weight_ref, s_ref, inflow_ref, response_ref, below_ref, rims_ref, edges_ref,
    flat, sea, columns, field, state, closing, keeps, laps, starts, rates,
    ew, gathered, ab, edge, edges_in, rim, rims_in, constants, others, lat_first, lat_second, inflow_in,
    ew_send, ew_sem, edge_send, edge_sem, rim_send, rim_sem,
    rate_send, rate_sem, share_send, share_sem, reply_send, reply_sem, out_sem,
):
    step = pl.program_id(0)
    lat, lon = lax.axis_index("lat"), lax.axis_index("lon")
    barrier = pltpu.get_barrier_semaphore()

    def remote(source, target, send, recv, to):
        return pltpu.make_async_remote_copy(
            src_ref=source, dst_ref=target, send_sem=send, recv_sem=recv, device_id=to, device_id_type=MESH
        )

    def lon_peer(k):
        return lax.rem(lon + k, LON)

    def lat_peer(k):
        return lax.rem(lat + k, LAT)

    def each(count, act):
        lax.fori_loop(1, count, lambda k, c: (act(k), c)[1], 0)

    def closing_copy(band, to, slot):
        return remote(ew.at[band], gathered.at[band, slot], ew_send.at[band, to], ew_sem.at[band, slot], (lat, to))

    def edge_copy(side):
        to = lon_peer(LON - 1 if side == 0 else 1)
        return remote(edge.at[side], edges_in.at[1 - side], edge_send.at[side], edge_sem.at[1 - side], (lat, to))

    def rim_copy(side):
        to = lat_peer(LAT - 1 if side == 0 else 1)
        return remote(rim.at[side], rims_in.at[1 - side], rim_send.at[side], rim_sem.at[1 - side], (to, lon))

    def rate_copy(to, slot):
        return remote(constants, others.at[slot], rate_send.at[to], rate_sem.at[slot], (to, lon))

    def part(index):
        return pl.ds(pl.multiple_of(index * SHARE, 8), SHARE)

    def share_copy(side, index, slot):
        return remote(
            closing.at[side, part(index)], lat_first.at[slot, side],
            share_send.at[side, index], share_sem.at[side, slot], (index, lon),
        )

    def share_arrival(side, slot):
        return remote(
            lat_first.at[slot, side], lat_first.at[slot, side],
            share_send.at[side, slot], share_sem.at[side, slot], (slot, lon),
        )

    def reply_copy(side, to, index):
        return remote(
            lat_second.at[to, side], inflow_in.at[side, part(index)],
            reply_send.at[side, to], reply_sem.at[side, index], (to, lon),
        )

    def far_lat(k):
        return lat_peer(lax.rem(k + 2, LAT - 1) + 1)

    def far_lon(k):
        return lon_peer(lax.rem(k + 6, LON - 1) + 1)

    def out_copy(index):
        return pltpu.make_async_copy(field.at[:, part(index)], s_ref.at[:, part(index)], out_sem.at[index])

    zero = jnp.zeros((8, LANES), F32)
    ones = jnp.ones((8, LANES), F32)

    @pl.when(step == 0)
    def _():
        each(LON, lambda k: pl.semaphore_signal(barrier, inc=1, device_id=(lat, lon_peer(k)), device_id_type=MESH))
        each(LAT, lambda k: pl.semaphore_signal(barrier, inc=1, device_id=(lat_peer(k), lon), device_id_type=MESH))
        flat[...] = jnp.zeros_like(flat)
        columns[EXTENT * ROW_PITCH :] = jnp.zeros(((PADDED - EXTENT) * ROW_PITCH, LANES), F32)
        state[...] = jnp.zeros_like(state)
        for block in range(ROWS // 8):
            keep = row_keep(class_ref, rate_ref, block * 8, 8)
            keeps[block * 8 : block * 8 + 8] = keep
            q = keep * keep
            q4 = q * q
            q8 = q4 * q4
            q256 = q8
            for _ in range(5):
                q256 = q256 * q256
            laps[block * 8 : block * 8 + 8] = q256 * q8 * q4 * q
        decay = class_decay(rate_ref)
        log_keep = jnp.log(1.0 - decay)
        rates[0] = decay * jnp.sqrt(decay / (2.0 - decay))
        rates[1] = jnp.exp(log_keep * 8.0)
        rates[2] = jnp.exp(log_keep * (SECTOR + 1.0))
        row = lax.broadcasted_iota(jnp.int32, (8, LANES), 0).astype(F32)
        for entry in range(CLASSES):
            log = log_keep[entry : entry + 1]
            for index in range(SHARES):
                starts[index, entry, 0] = jnp.exp(log * (row + (SHARE * index + 1.0)))
                starts[index, entry, 1] = jnp.exp(log * (SECTOR + 8.0 - SHARE * (index + 1.0) - row))

        def onward(i, unit):
            unit = jnp.broadcast_to(keeps[pl.ds(i, 1), :], (8, LANES)) * unit
            response_ref[0, pl.ds(i, 1), :] = unit[:1]
            return unit

        product = lax.fori_loop(0, ROWS, onward, ones, unroll=4)

        def back(k, carried):
            unit, inflow = carried
            i = ROWS - 1 - k
            keep = jnp.broadcast_to(keeps[pl.ds(i, 1), :], (8, LANES))
            unit = keep * unit + (1.0 - keep) * jnp.broadcast_to(response_ref[0, pl.ds(i, 1), :], (8, LANES))
            inflow = keep * inflow
            response_ref[0, pl.ds(i, 1), :] = unit[:1]
            response_ref[1, pl.ds(i, 1), :] = inflow[:1]
            return unit, inflow

        unit, _ = lax.fori_loop(0, ROWS, back, (zero, ones), unroll=4)
        at = lax.broadcasted_iota(jnp.int32, (8, LANES), 0)
        last = jnp.broadcast_to(keeps[ROWS - 1 :], (8, LANES))
        tile = jnp.where(at == 0, product, unit)
        tile = jnp.where(at == 2, last, tile)
        constants[...] = jnp.where(at == 3, 1.0 - last, tile)

    for level in range(LEVELS):
        for half in range(BAND // 8):
            for block in range(BLOCKS):
                weight = block_of(mask_ref, level, pl.ds(half * 8, 8), block).astype(F32)
                for group in range(4):
                    place = half * 8 * PITCH + group * LEVELS + level
                    flat[block, pl.ds(place, 8, stride=PITCH), :] = weight

    eye = identity(2 * LANES)
    small = eye[:16, :LANES]

    def pair(k, _):
        at = [pl.ds(pl.multiple_of((2 * k + n) * PITCH, 8), LANES) for n in range(2)]
        parts = [
            jnp.concatenate([flat[b, at[n], :] for n in range(2)], axis=0).astype(BF16)
            for b in range(BLOCKS)
        ]
        main = transposed_dot(eye, jnp.concatenate(parts[:2], axis=1))
        tail = transposed_dot(small, parts[2])
        for n in range(2):
            whole = jnp.concatenate(
                [main[:, n * LANES : (n + 1) * LANES], tail[:, n * LANES : (n + 1) * LANES]], axis=0
            )
            row = 2 * k + n
            weight_ref[row] = whole.astype(BF16)
            for t in range(EXTENT // 8):
                sea[pl.ds(t * 8 * SEA_PITCH + row, 8, stride=SEA_PITCH), :] = whole[t * 8 : t * 8 + 8]
        return 0

    lax.fori_loop(0, BAND // 2, pair, 0, unroll=8)

    here = pl.ds(pl.multiple_of(step * BAND, BAND), BAND)
    edge[0, here] = sea[:BAND]
    edge[1, here] = sea[(SECTOR - 1) * SEA_PITCH : (SECTOR - 1) * SEA_PITCH + BAND]

    keep = keeps[here]
    keep2 = keep * keep

    def taken(j):
        inside = sea[pl.ds(pl.multiple_of(j * SEA_PITCH, 8), BAND), :] != 0.0
        return jnp.where(inside, widened(control_ref[j]), 0.0)

    def spot(j):
        return pl.ds(pl.multiple_of(j * ROW_PITCH + step * BAND, 8), BAND)

    def advance(p, carried, add_east, add_west):
        east, west = carried
        j, k = 2 * p, SECTOR - 1 - 2 * p
        x0, x1 = taken(j), taken(j + 1)
        z0, z1 = taken(k), taken(k - 1)
        mid = keep * x0 + x1
        e0 = keep * east + x0
        e1 = keep2 * east + mid
        if add_east:
            columns[spot(j)] = columns[spot(j)] + e0
            columns[spot(j + 1)] = columns[spot(j + 1)] + e1
        else:
            columns[spot(j)] = e0
            columns[spot(j + 1)] = e1
        w0 = keep * west
        w1 = keep2 * west + keep * z0
        if add_west:
            columns[spot(k)] = columns[spot(k)] + w0
            columns[spot(k - 1)] = columns[spot(k - 1)] + w1
        else:
            columns[spot(k)] = w0
            columns[spot(k - 1)] = w1
        return e1, keep2 * west + (keep * z0 + z1)

    nothing = jnp.zeros((BAND, LANES), F32)
    pairs = SECTOR // 2
    carried = lax.fori_loop(
        0, pairs // 2 - 1, lambda p, c: advance(p, c, False, False), (nothing, nothing), unroll=6
    )
    carried = advance(pairs // 2 - 1, carried, False, False)
    carried = advance(pairs // 2, carried, False, True)
    carried = lax.fori_loop(
        pairs // 2 + 1, pairs - 1, lambda p, c: advance(p, c, True, True), carried, unroll=6
    )
    east, west = advance(pairs - 1, carried, True, True)
    columns[spot(SECTOR)] = keep * east
    columns[spot(SECTOR + 1)] = keep * west

    @pl.when(step == 0)
    def _():
        rim[0] = weight_ref[0].astype(F32)
        pl.semaphore_wait(barrier, LON + LAT - 2)
        each(LAT, lambda k: rate_copy(lat_peer(k), lat).start())
        others[lat] = constants[...]
        rim_copy(0).start()

    for half in range(BAND // 8):
        for side, value in enumerate((east, west)):
            ew[step, 2 * half + side] = value[half * 8 : half * 8 + 8]
    each(LON, lambda k: closing_copy(step, far_lon(k), lon).start())
    gathered[step, lon] = ew[step]

    @pl.when(step == BANDS - 1)
    def _():
        rim[1] = weight_ref[BAND - 1].astype(F32)
        edge_copy(0).start()
        edge_copy(1).start()
        rim_copy(1).start()

    special = lax.broadcasted_iota(jnp.int32, (8, LANES), 0) == 7

    def forward_band(band, _):
        each(LON, lambda k: closing_copy(band, lon_peer(k), lon_peer(k)).wait_recv())
        for half in range(BAND // 8):
            q = laps[pl.ds(pl.multiple_of(band * BAND + half * 8, 8), 8)]
            whole = q
            for _ in range(4):
                whole = whole * whole
            part_of = 1.0 / (1.0 - whole)

            def gather(k, carried):
                a, b = carried
                a = q * a + gathered[band, lon_peer(k), 2 * half]
                b = q * b + gathered[band, lon_peer(LON - k), 2 * half + 1]
                return a, b

            a, b = lax.fori_loop(0, LON, gather, (zero, zero), unroll=4)
            ab[2 * half] = a * part_of
            ab[2 * half + 1] = b * part_of

        def strip(index, _):
            final = special & (jnp.full((8, LANES), index) == SHARES - 1)
            base = pl.multiple_of(index * SHARE, 8)

            def one_row(ii, north):
                row = band * BAND + ii
                entry = class_ref[row]
                keep = 1.0 - rate_ref[entry]
                gain, stride8, far = [
                    jnp.broadcast_to(rates[n, pl.ds(entry, 1), :], (8, LANES)) for n in range(3)
                ]
                at = ii // 8 * 2
                a = jnp.broadcast_to(ab[at, pl.ds(row % 8, 1), :], (8, LANES))
                b = jnp.broadcast_to(ab[at + 1, pl.ds(row % 8, 1), :], (8, LANES))
                ahead = [a * starts[index, entry, 0]]
                behind = [b * starts[index, entry, 1]]
                for _ in range(TILES - 1):
                    ahead.append(ahead[-1] * stride8)
                    behind.append(behind[-1] * stride8)
                behind = behind[::-1]
                ahead[3] = jnp.where(final, a, ahead[3])
                behind[3] = jnp.where(final, b * far, behind[3])
                done = []
                for t in range(TILES):
                    y = columns[pl.ds((base + t * 8) * ROW_PITCH + row, 8, stride=ROW_PITCH), :]
                    done.append(keep * north[t] + gain * (y + ahead[t] + behind[t]))
                    field[row, pl.ds(base + t * 8, 8), :] = done[t]
                return tuple(done)

            north = tuple(state[pl.ds(base + t * 8, 8), :] for t in range(TILES))
            north = lax.fori_loop(0, BAND, one_row, north, unroll=16)
            for t in range(TILES):
                state[pl.ds(base + t * 8, 8), :] = north[t]
            return 0

        lax.fori_loop(0, SHARES, strip, 0)
        return 0

    @pl.when(step == BANDS - 1)
    def _():
        lax.fori_loop(0, BANDS, forward_band, 0)
        closing[0] = state[...]

        def send_north(k, c):
            index = lax.rem(lat + 1 + k, SHARES)

            @pl.when(index != lat)
            def _():
                share_copy(0, index, lat).start()

            @pl.when(index == lat)
            def _():
                lat_first[lat, 0] = closing[0, part(lat)]

            return c

        lax.fori_loop(0, SHARES, send_north, 0)
        each(LAT, lambda k: rate_copy(lat_peer(k), lat_peer(k)).wait_recv())

        def strip(turn, _):
            index = lax.rem(lat + 1 + turn, SHARES)
            base = pl.multiple_of(index * SHARE, 8)

            def one_row(k, south):
                row = ROWS - 1 - k
                decay = rate_ref[class_ref[row]]
                keep = 1.0 - decay
                done = []
                for t in range(TILES):
                    at = pl.ds(base + t * 8, 8)
                    done.append(keep * south[t] + decay * field[row, at, :])
                    field[row, at, :] = done[t]
                return tuple(done)

            south = lax.fori_loop(0, ROWS, one_row, (zero,) * TILES, unroll=4)
            for t in range(TILES):
                closing[1, pl.ds(base + t * 8, 8), :] = south[t]
            out_copy(index).start()

            @pl.when(index != lat)
            def _():
                share_copy(1, index, lat).start()

            @pl.when(index == lat)
            def _():
                lat_first[lat, 1] = closing[1, part(lat)]

            @pl.when((lat < SHARES) & (turn == SHARES - 2))
            def _():
                each(LAT, lambda k: share_arrival(0, lat_peer(k)).wait_recv())
                lat_second[0, 0] = jnp.zeros((SHARE, LANES), F32)
                for t in range(LAT - 1):
                    lat_second[t + 1, 0] = lat_first[t, 0] + others[t, 0:1, :] * lat_second[t, 0]
                each(LAT, lambda k: reply_copy(0, far_lat(k), lat).start())
                inflow_in[0, part(lat)] = lat_second[lat, 0]

            @pl.when((lat < SHARES) & (turn == SHARES - 1))
            def _():
                each(LAT, lambda k: share_arrival(1, lat_peer(k)).wait_recv())
                lat_second[LAT - 1, 1] = jnp.zeros((SHARE, LANES), F32)
                for t in range(LAT - 1, 0, -1):
                    lat_second[t - 1, 1] = (
                        lat_first[t, 1]
                        + others[t, 1:2, :] * lat_second[t, 0]
                        + others[t, 0:1, :] * lat_second[t, 1]
                    )
                each(LAT, lambda k: reply_copy(1, far_lat(k), lat).start())
                inflow_in[1, part(lat)] = lat_second[lat, 1]

            return 0

        lax.fori_loop(0, SHARES, strip, 0)
        edge_copy(0).wait()
        edge_copy(1).wait()
        rim_copy(0).wait()
        rim_copy(1).wait()
        edges_ref[...] = edges_in[...]
        rims_ref[...] = rims_in[...]
        below_ref[...] = others[lat_peer(LAT - 1)] * (lat > 0).astype(F32)
        for band in range(BANDS):
            each(LON, lambda k: closing_copy(band, lon_peer(k), lon).wait_send())
        each(LAT, lambda k: rate_copy(lat_peer(k), lat).wait_send())

        def settle(index, c):
            @pl.when(index != lat)
            def _():
                for side in range(2):
                    share_copy(side, index, lat).wait_send()
                    reply_copy(side, index, index).wait_recv()

            out_copy(index).wait()
            return c

        lax.fori_loop(0, SHARES, settle, 0)

        @pl.when(lat < SHARES)
        def _():
            for side in range(2):
                each(LAT, lambda k: reply_copy(side, lat_peer(k), lat).wait_send())

        inflow_ref[...] = inflow_in[...]


def final_kernel(
    s_ref, weight_ref, mask_ref, inflow_ref, response_ref, below_ref, rims_ref, edges_ref, balance_ref,
    increment_ref, velocity_ref, mixer, picker, padded, mixed, sea, pressure, kept, factor,
):
    step = pl.program_id(0)
    lane = lane_iota(8)

    @pl.when(step == 0)
    def _():
        padded[...] = jnp.zeros_like(padded)
        padded[:COMP, :COMP] = balance_ref[...]
        high, low = split(padded[:LANES])
        mixer[:LANES, :LANES] = high
        mixer[:LANES, LANES:] = high
        mixer[LANES:, :LANES] = low
        mixer[LANES:, LANES:] = jnp.zeros_like(low)
        high, low = split(padded[COMP - LEVELS : COMP - LEVELS + 32])
        picker[:32, :LANES] = high
        picker[:32, LANES:] = high
        picker[32:, :LANES] = low
        picker[32:, LANES:] = jnp.zeros_like(low)
        row = lax.axis_index("lat") * ROWS + lax.broadcasted_iota(jnp.int32, (ROWS, LANES), 0)
        latitude = (-70.0 + 140.0 * (row.astype(F32) + 0.5) / 512.0) * (math.pi / 180.0)
        sine = jnp.sin(latitude)
        factor[...] = 0.5 * (sine / (sine * sine + 0.01))

    def operand(field):
        high, low = split(field)
        return jnp.concatenate([high, low], axis=1)

    def pressures(both):
        product = transposed_dot(picker[...], both)
        total = product[:32] + product[32:]
        end = jnp.concatenate([total[:, 2 * LANES :], jnp.zeros((32, 3 * LANES - EXTENT), F32)], axis=1)
        return [total[:, :LANES], total[:, LANES : 2 * LANES], end]

    def rim_row(field, side, row):
        rim = rims_ref[side]
        result = pressures(operand(field * rim))
        shown = transposed_dot(identity(LANES)[:32], rim.astype(BF16))
        shown = jnp.concatenate([shown, jnp.zeros((32, 3 * LANES - EXTENT), F32)], axis=1)
        for b in range(BLOCKS):
            pressure[b, row * PRESSURE_PITCH : row * PRESSURE_PITCH + 32, :] = (
                result[b] * shown[:, b * LANES : (b + 1) * LANES]
            )

    @pl.when(step == 0)
    def _():
        north, south = inflow_ref[0, :EXTENT], inflow_ref[1, :EXTENT]
        first = s_ref[0] + response_ref[0, 0:1, :] * north + response_ref[1, 0:1, :] * south
        rim_row(below_ref[2:3, :] * first + below_ref[3:4, :] * north, 0, 0)

    @pl.when(step == ROWS // 8)
    def _():
        rim_row(inflow_ref[1, :EXTENT], 1, ROWS + 1)

    @pl.when(step < ROWS // 8)
    def _():
        rows = pl.ds(pl.multiple_of(step * 8, 8), 8)
        west, east = edges_ref[0, rows], edges_ref[1, rows]
        for level in range(LEVELS):
            for block in range(BLOCKS):
                weight = block_of(mask_ref, level, pl.ds(0, 8), block).astype(F32)
                if block == BLOCKS - 1:
                    weight = jnp.where(lane == TAIL, lane_of(east, level), weight)
                    weight = jnp.where(lane == TAIL + 1, lane_of(west, level), weight)
                kept[step % 2, level, :, pl.ds(block * LANES, LANES)] = weight
                sea[block, pl.ds(level, 8, stride=PRESSURE_PITCH), :] = weight

        def one_row(i, _):
            row = step * 8 + i
            h, p = response_ref[0, pl.ds(row, 1), :], response_ref[1, pl.ds(row, 1), :]
            tail = lax.broadcasted_iota(jnp.int32, (8, LANES), 0)
            weight = weight_ref[i].astype(F32)
            e, w = edges_ref[1, pl.ds(row, 1), :], edges_ref[0, pl.ds(row, 1), :]
            end = jnp.where(tail == 6, e, jnp.where(tail == 7, w, weight[EXTENT - 8 :]))
            weight = jnp.concatenate([weight[: EXTENT - 8], end], axis=0)
            field = s_ref[i] + h * inflow_ref[0, :EXTENT] + p * inflow_ref[1, :EXTENT]
            both = operand(field * weight)
            product = transposed_dot(both, mixer[...])
            total = (product[:, :LANES] + product[:, LANES:]) * weight
            for t in range(EXTENT // 8):
                mixed[pl.ds(t * 64 + i, 8, stride=8), :] = total[t * 8 : t * 8 + 8]
            result = pressures(both)
            at = pl.multiple_of((row + 1) * PRESSURE_PITCH, 8)
            for b in range(BLOCKS):
                pressure[b, pl.ds(at, 32), :] = (
                    result[b] * sea[b, pl.ds(pl.multiple_of(i * PRESSURE_PITCH, 8), 32), :]
                )
            return 0

        lax.fori_loop(0, 8, one_row, 0, unroll=8)

        def place(j, _):
            increment_ref[j] = mixed[pl.ds(pl.multiple_of(j * 8, 8), 8), :COMP]
            return 0

        lax.fori_loop(0, SECTOR, place, 0, unroll=27)

    @pl.when(step > 0)
    def _():
        done = step - 1
        base = done * (8 * PRESSURE_PITCH)
        scale = factor[pl.ds(pl.multiple_of(done * 8, 8), 8)]
        for level in range(LEVELS):
            centre = []
            for block in range(BLOCKS):
                below, here, above = [
                    pressure[block, pl.ds(base + k * PRESSURE_PITCH + level, 8, stride=PRESSURE_PITCH), :]
                    for k in range(3)
                ]
                centre.append(here)
                weight = kept[(step + 1) % 2, level, :, pl.ds(block * LANES, LANES)]
                place_block(velocity_ref, 0, level, block, -scale * (above - below) * weight)
            ups = [pltpu.roll(c, LANES - 1, 1) for c in centre]
            downs = [pltpu.roll(c, 1, 1) for c in centre]
            wrap = pltpu.roll(centre[2], LANES - TAIL - 1, 1)
            for block in range(BLOCKS):
                right = ups[block]
                if block < BLOCKS - 1:
                    right = jnp.where(lane == LANES - 1, ups[block + 1], right)
                left = jnp.where(lane == 0, downs[block - 1] if block else wrap, downs[block])
                weight = kept[(step + 1) % 2, level, :, pl.ds(block * LANES, LANES)]
                place_block(velocity_ref, 1, level, block, scale * (right - left) * weight)


def body(control, land_mask, row_class, decay_rate, balance):
    wide = BLOCKS * LANES
    params = functools.partial(pltpu.CompilerParams, vmem_limit_bytes=LIMIT)

    def like(*shape):
        return jax.ShapeDtypeStruct(shape, F32)

    columns = jnp.transpose(control, (2, 1, 0))

    dma = pltpu.SemaphoreType.DMA
    fixed2, fixed3 = (lambda g: (0, 0)), (lambda g: (0, 0, 0))
    weight, s, inflow, response, below, rims, edges = pl.pallas_call(
        analysis_kernel,
        grid=(BANDS,),
        in_specs=[
            SMEM,
            SMEM,
            pl.BlockSpec((SECTOR, BAND, COMP), lambda g: (0, g, 0)),
            pl.BlockSpec((LEVELS, BAND, SECTOR), lambda g: (0, g, 0)),
        ],
        out_specs=[
            pl.BlockSpec((BAND, EXTENT, LANES), lambda g: (g, 0, 0)),
            pl.BlockSpec(memory_space=pl.ANY),
            pl.BlockSpec((2, PADDED, LANES), fixed3),
            pl.BlockSpec((2, ROWS, LANES), fixed3),
            pl.BlockSpec((8, LANES), fixed2),
            pl.BlockSpec((2, EXTENT, LANES), fixed3),
            pl.BlockSpec((2, ROWS, LANES), fixed3),
        ],
        out_shape=[
            pltpu.VMEM((ROWS, EXTENT, LANES), BF16),
            pltpu.VMEM((ROWS, PADDED, LANES), F32),
            pltpu.VMEM((2, PADDED, LANES), F32),
            pltpu.VMEM((2, ROWS, LANES), F32),
            pltpu.VMEM((8, LANES), F32),
            pltpu.VMEM((2, EXTENT, LANES), F32),
            pltpu.VMEM((2, ROWS, LANES), F32),
        ],
        scratch_shapes=[
            pltpu.VMEM((BLOCKS, BAND * PITCH, LANES), F32),
            pltpu.VMEM((EXTENT * SEA_PITCH, LANES), F32),
            pltpu.VMEM((PADDED * ROW_PITCH, LANES), F32),
            pltpu.VMEM((ROWS, PADDED, LANES), F32),
            pltpu.VMEM((PADDED, LANES), F32),
            pltpu.VMEM((2, PADDED, LANES), F32),
            pltpu.VMEM((ROWS, LANES), F32),
            pltpu.VMEM((ROWS, LANES), F32),
            pltpu.VMEM((SHARES, CLASSES, 2, 8, LANES), F32),
            pltpu.VMEM((3, CLASSES, LANES), F32),
            pltpu.VMEM((BANDS, 4, 8, LANES), F32),
            pltpu.VMEM((BANDS, LON, 4, 8, LANES), F32),
            pltpu.VMEM((4, 8, LANES), F32),
            pltpu.VMEM((2, ROWS, LANES), F32),
            pltpu.VMEM((2, ROWS, LANES), F32),
            pltpu.VMEM((2, EXTENT, LANES), F32),
            pltpu.VMEM((2, EXTENT, LANES), F32),
            pltpu.VMEM((8, LANES), F32),
            pltpu.VMEM((LAT, 8, LANES), F32),
            pltpu.VMEM((LAT, 2, SHARE, LANES), F32),
            pltpu.VMEM((LAT, 2, SHARE, LANES), F32),
            pltpu.VMEM((2, PADDED, LANES), F32),
            dma((BANDS, LON)),
            dma((BANDS, LON)),
            dma((2,)),
            dma((2,)),
            dma((2,)),
            dma((2,)),
            dma((LAT,)),
            dma((LAT,)),
            dma((2, LAT)),
            dma((2, LAT)),
            dma((2, LAT)),
            dma((2, LAT)),
            dma((SHARES,)),
        ],
        compiler_params=params(collective_id=0, has_side_effects=True),
        name="analysis",
    )(row_class, decay_rate, columns, land_mask)

    increment, velocity = pl.pallas_call(
        final_kernel,
        grid=(ROWS // 8 + 1,),
        in_specs=[
            pl.BlockSpec((8, EXTENT, LANES), lambda g: (jnp.minimum(g, 7), 0, 0)),
            pl.BlockSpec((8, EXTENT, LANES), lambda g: (jnp.minimum(g, 7), 0, 0)),
            pl.BlockSpec((LEVELS, 8, SECTOR), lambda g: (0, jnp.minimum(g, 7), 0)),
            *[VMEM] * 6,
        ],
        out_specs=[
            pl.BlockSpec((SECTOR, 8, COMP), lambda g: (0, jnp.minimum(g, 7), 0)),
            pl.BlockSpec((2, LEVELS, 8, SECTOR), lambda g: (0, 0, jnp.maximum(g - 1, 0), 0)),
        ],
        out_shape=[like(SECTOR, ROWS, COMP), like(2, LEVELS, ROWS, SECTOR)],
        scratch_shapes=[
            pltpu.VMEM((2 * LANES, 2 * LANES), BF16),
            pltpu.VMEM((64, 2 * LANES), BF16),
            pltpu.VMEM((LANES, LANES), F32),
            pltpu.VMEM((EXTENT * 8, LANES), F32),
            pltpu.VMEM((BLOCKS, 8 * PRESSURE_PITCH, LANES), F32),
            pltpu.VMEM((BLOCKS, (ROWS + 2) * PRESSURE_PITCH, LANES), F32),
            pltpu.VMEM((2, LEVELS, 8, wide), F32),
            pltpu.VMEM((ROWS, LANES), F32),
        ],
        compiler_params=pltpu.CompilerParams(vmem_limit_bytes=24 * 1024 * 1024),
        name="final",
    )(s, weight, land_mask, inflow, response, below, rims, edges, balance)
    return jnp.transpose(increment, (2, 1, 0)), velocity


def solution(mesh):
    return jax.shard_map(
        body,
        mesh=mesh,
        in_specs=(P(None, "lat", "lon"), P(None, "lat", "lon"), P("lat"), P(), P()),
        out_specs=(P(None, "lat", "lon"), P(None, None, "lat", "lon")),
        check_vma=False,
    )
```
